256 devices in a mesh: row: 64 (over z, x, core), col: 4 (over y).
Axes of the slice: x: 4, y: 4, z: 8, core: 2. Of those that a mesh axis runs over, the one named last changes fastest.
Arguments:
- rhs: float32 [512, 72, 64], P('row', None, 'col'), may hold values from -60 to 60
- system_lower: float32 [512, 8, 72, 72], P('row', 'col'), may hold values from -0.625 to 0.625
- system_diag: float32 [512, 72, 72], P('row'), may hold values from -16 to 20, as said below
- factor_lower: float32 [512, 8, 72, 72], P('row'), may hold values from -0.4375 to 0.4375
- diag_inverse: float32 [512, 72, 72], P('row'), may hold values from -0.25 to 2, as said below
- neighbours: int32 [512, 8], P('row'), may hold values from -1 to 510, as said below
- counts: int32 [512], P('row'), may hold values from 0 to 8, as said below
Outputs:
- solution: float32 [512, 72, 64], P('row', None, 'col')
- residual: float32 [512, 72, 64], P('row', None, 'col')
- direction: float32 [512, 72, 64], P('row', None, 'col')
The draws below stay inside these ranges and needn't reach their ends.
Inputs may be any that keep to these rules, and one draw needn't show every extreme that they name: `neighbours`: block rows come in aligned groups of 8. Entries k < counts[i] of row i name distinct block rows j < i that lie in the group of i or are the last two block rows of the group before; entry 0 is i - 1 for every i >= 1; all other entries are -1. `counts`: block row 0 has no neighbours, every other block row at least one, and the last block row of every group but the first has 8. `diag_inverse`: each block is lower triangular with its diagonal entries between 0.5 and 2. `system_diag`: each block is symmetric positive definite.
All inputs are finite; a program needn't handle non-finite values.
Results may differ from the reference program's by a relative error of at most 0.0003.
Values sent between devices are 32-bit elements; how exact they have to be, the bound alone decides.
A program may use at most 64 MiB of HBM per device.

```python
import math
import jax
import jax.numpy as jnp
from jax import lax

BLK = 72
SLOTS = 8
ROWS_BLK = 8
ITERS = 2
NB = 512
RHS = 64


def pattern(key):
    key = jax.random.fold_in(key, 101)
    order_key, count_key = jax.random.split(key)
    glob = jnp.arange(NB, dtype=jnp.int32)
    device = glob // ROWS_BLK
    place = glob % ROWS_BLK
    candidate = jnp.arange(ROWS_BLK + 2, dtype=jnp.int32)
    valid_rim = (candidate[None, :] < 2) & (device[:, None] > 0)
    valid_local = (candidate[None, :] >= 2) & (candidate[None, :] - 2 < place[:, None])
    valid = valid_rim | valid_local
    random_part = jax.random.randint(order_key, (NB, ROWS_BLK + 2), 0, 2 ** 20, dtype=jnp.int32)
    score = random_part * 128 + candidate[None, :]
    is_previous = candidate[None, :] == place[:, None] + 1
    score = jnp.where(is_previous, score + 2 ** 29, score)
    score = jnp.where(valid, score, -1 - candidate[None, :])
    _, order = lax.top_k(score, SLOTS)
    ident = device[:, None] * ROWS_BLK - 2 + order.astype(jnp.int32)
    number_valid = jnp.sum(valid.astype(jnp.int32), axis=1)
    drawn = jax.random.randint(count_key, (NB,), 1, SLOTS + 1, dtype=jnp.int32)
    drawn = jnp.where((place == ROWS_BLK - 1) & (device > 0), SLOTS, drawn)
    count = jnp.minimum(drawn, number_valid).astype(jnp.int32)
    slot = jnp.arange(SLOTS, dtype=jnp.int32)
    named = jnp.where(slot[None, :] < count[:, None], ident, -1).astype(jnp.int32)
    return (named, count)


def draw_neighbours(key, part):
    return pattern(key)[0]


def draw_counts(key, part):
    return pattern(key)[1]


def draw_rhs(key, part):
    key = jax.random.fold_in(key, 202)
    base_key, row_key, col_key = jax.random.split(key, 3)
    rise = 1.0 + 2.0 * jnp.arange(NB, dtype=jnp.float32) / max(NB - 1, 1)
    row_scale = jnp.exp(jax.random.uniform(row_key, (NB,), jnp.float32, 0.0, math.log(10.0)))
    col_scale = jnp.exp(jax.random.uniform(col_key, (RHS,), jnp.float32, 0.0, math.log(10.0)))
    base = jax.random.truncated_normal(base_key, -4.0, 4.0, (NB, BLK, RHS), jnp.float32)
    return base * (rise * row_scale)[:, None, None] * col_scale[None, None, :] / 20.0


def draw_system_diag(key, part):
    key = jax.random.fold_in(key, 303)
    left_key, diag_key = jax.random.split(key)
    factor = jax.random.truncated_normal(left_key, -4.0, 4.0, (NB, BLK, BLK), jnp.float32)
    lift = jnp.exp(jax.random.uniform(diag_key, (NB, BLK), jnp.float32, math.log(0.5), math.log(4.0)))
    gram = jnp.einsum('nab,ncb->nac', factor, factor) / BLK
    gram = 0.5 * (gram + jnp.swapaxes(gram, 1, 2))
    return gram + lift[:, :, None] * jnp.eye(BLK, dtype=jnp.float32)[None, :, :]


def draw_diag_inverse(key, part):
    key = jax.random.fold_in(key, 404)
    diag_key, off_key = jax.random.split(key)
    diagonal = jnp.exp(jax.random.uniform(diag_key, (NB, BLK), jnp.float32, math.log(0.5), math.log(2.0)))
    below = jax.random.truncated_normal(off_key, -4.0, 4.0, (NB, BLK, BLK), jnp.float32) * 0.06
    strict = jnp.tril(below, -1)
    return strict + diagonal[:, :, None] * jnp.eye(BLK, dtype=jnp.float32)[None, :, :]


def levels(rng, shape, shards, low, high):
    level = 1.0
    for position, parts in shards:
        draws = jax.random.uniform(jax.random.fold_in(jax.random.fold_in(rng, 6), position), (parts,), jnp.float32, low / len(shards), high / len(shards))
        level = level * jnp.repeat(jnp.exp(draws), shape[position] // parts).reshape((-1,) + (1,) * (len(shape) - 1 - position))
    return level


def centred(key, extent, deviation, limit, cuts=(), kind=jnp.bfloat16):
    values = jax.random.normal(key, extent, jnp.float32) * deviation
    if len(cuts) > 0:
        values = levels(key, extent, cuts, -0.22, 0.18) * values
    return jnp.clip(values, min=-limit, max=limit).astype(kind)


def setup_inputs(seed: int = 0) -> dict:
    seeds = jax.random.split(jax.random.key(seed), 8)
    return {
        "rhs": draw_rhs(jax.random.fold_in(seeds[7], 71), 0),
        "system_lower": centred(seeds[1], (NB, SLOTS, BLK, BLK), 0.04, 0.625, ((0, 64), (1, 4)), jnp.float32),
        "system_diag": draw_system_diag(jax.random.fold_in(seeds[7], 71), 0),
        "factor_lower": centred(seeds[3], (NB, SLOTS, BLK, BLK), 0.03, 0.4375, ((0, 64),), jnp.float32),
        "diag_inverse": draw_diag_inverse(jax.random.fold_in(seeds[7], 71), 0),
        "neighbours": draw_neighbours(jax.random.fold_in(seeds[7], 71), 0),
        "counts": draw_counts(jax.random.fold_in(seeds[7], 71), 0),
    }


HIGH = lax.Precision.HIGHEST


def slot_mask(counts):
    return (jnp.arange(SLOTS, dtype=jnp.int32)[None, :] < counts[:, None]).astype(jnp.float32)


def system_times(system_lower, system_diag, neighbours, counts, vector):
    live = slot_mask(counts)
    safe = jnp.maximum(neighbours, 0).astype(jnp.int32)
    shares = jnp.einsum("nkab,nac->nkbc", system_lower, vector, precision=HIGH) * live[:, :, None, None]
    upper = jnp.zeros_like(vector).at[safe.reshape(-1)].add(shares.reshape(-1, BLK, RHS))
    inner = vector + upper
    picked = inner[safe] * live[:, :, None, None]
    lower = jnp.einsum("nkab,nkbc->nac", system_lower, picked, precision=HIGH)
    diagonal_part = jnp.einsum("nab,nbc->nac", system_diag, vector, precision=HIGH)
    return diagonal_part + inner + lower


def precondition(factor_lower, diag_inverse, neighbours, counts, residual):
    live = slot_mask(counts)
    safe = jnp.maximum(neighbours, 0).astype(jnp.int32)

    def forward(buffer, row):
        picked = buffer[safe[row]] * live[row][:, None, None]
        gathered_sum = jnp.einsum("kab,kbc->ac", factor_lower[row], picked, precision=HIGH)
        value = jnp.dot(diag_inverse[row], residual[row] - gathered_sum, precision=HIGH)
        return buffer.at[row].set(value), None

    solved, _ = lax.scan(forward, jnp.zeros_like(residual), jnp.arange(NB, dtype=jnp.int32))

    def backward(carried, row):
        value = jnp.dot(diag_inverse[row].T, solved[row] - carried[row], precision=HIGH)
        shares = jnp.einsum("kab,ac->kbc", factor_lower[row], value, precision=HIGH) * live[row][:, None, None]
        carried = carried.at[safe[row]].add(shares)
        return carried, value

    _, values = lax.scan(backward, jnp.zeros_like(residual), jnp.arange(NB, dtype=jnp.int32), reverse=True)
    return values


def column_sum(left, right):
    return jnp.sum(left * right, axis=(0, 1))


def reference(rhs, system_lower, system_diag, factor_lower, diag_inverse, neighbours, counts):
    solution = jnp.zeros_like(rhs)
    residual = rhs
    precond = precondition(factor_lower, diag_inverse, neighbours, counts, residual)
    direction = precond
    energy = column_sum(residual, precond)
    for step in range(ITERS):
        image = system_times(system_lower, system_diag, neighbours, counts, direction)
        alpha = energy / column_sum(direction, image)
        solution = solution + alpha * direction
        residual = residual - alpha * image
        precond = precondition(factor_lower, diag_inverse, neighbours, counts, residual)
        energy_next = column_sum(residual, precond)
        direction = precond + (energy_next / energy) * direction
        energy = energy_next
    return solution, residual, direction
```

```python
import functools

import jax
import jax.numpy as jnp
from jax import lax
from jax.experimental import pallas as pl
from jax.experimental.pallas import tpu as pltpu
from jax.sharding import PartitionSpec as P

ITERS = 2
GROUP = 8
BLK = 72
ROWS = 8
PAD = 128
WIDE = ROWS * PAD
RIM = 2 * PAD
F32 = jnp.float32
BF16 = jnp.bfloat16
MESH = pl.DeviceIdType.MESH


def split(x):
    high = x.astype(BF16)
    return high, (x - high.astype(F32)).astype(BF16)


def dot(a, b, nt):
    return lax.dot_general(
        a, b, (((1,), (1 if nt else 0,)), ((), ())), preferred_element_type=F32
    )


def stacked(v):
    high, low = split(v)
    return jnp.concatenate([high, low], axis=0)


def few(vs, high, low, nt):
    rows = vs.shape[0] // 2
    both = dot(vs, high, nt)
    return both[:rows] + both[rows:] + dot(vs[:rows], low, nt)


def many(a, b, nt=False):
    return dot(a[0], b[0], nt) + (dot(a[0], b[1], nt) + dot(a[1], b[0], nt))


def kernel(
    span, spans, cols, mask_ref, rhs_ref, sysl_ref, sysd_ref, fac_ref, dinv_ref,
    sol_ref, res_ref, dir_ref,
    dense, xh, xl, lh, ll, dh, dl, gathered, abuf, bbuf, ah, al,
    mh, ml, rh, rl, nh, nl, ph, pq, m2h, m2l, n2h, n2l, ex, nbs, nbr,
    col_send, col_recv, a_send, a_recv, b_send, b_recv, ex_send, ex_recv, nb_send, nb_recv,
):
    row, col = lax.axis_index("row"), lax.axis_index("col")
    total = span * spans
    outer, inner = row // span, row % span
    share = sysl_ref.shape[1]
    columns = rhs_ref.shape[0]

    def inner_peer(t):
        return (outer * span + (inner + t) % span, col)

    def outer_peer(t):
        return (((outer + t) % spans) * span + inner, col)

    up, down = ((row + 1) % total, col), ((row + total - 1) % total, col)

    barrier = pltpu.get_barrier_semaphore()
    greeted = (
        [inner_peer(t) for t in range(1, span)]
        + [outer_peer(t) for t in range(1, spans)]
        + [(row, (col + t) % cols) for t in range(1, cols)]
        + [up, down]
    )
    for peer in greeted:
        pl.semaphore_signal(barrier, inc=1, device_id=peer, device_id_type=MESH)
    pl.semaphore_wait(barrier, len(greeted))

    sends = []

    def spread(buf, slot, peers, count, send_sem, recv_sem):
        for peer in peers:
            pltpu.make_async_remote_copy(
                src_ref=buf.at[slot], dst_ref=buf.at[slot], send_sem=send_sem,
                recv_sem=recv_sem, device_id=peer, device_id_type=MESH,
            ).start()
        every = pltpu.make_async_remote_copy(
            src_ref=buf.at[pl.ds(0, count)], dst_ref=buf.at[pl.ds(0, count)],
            send_sem=send_sem, recv_sem=recv_sem, device_id=up, device_id_type=MESH,
        )
        sends.append(every)
        return every

    for t in range(1, cols):
        pltpu.make_async_remote_copy(
            src_ref=sysl_ref, dst_ref=gathered.at[col], send_sem=col_send, recv_sem=col_recv,
            device_id=(row, (col + t) % cols), device_id_type=MESH,
        ).start()
    col_every = pltpu.make_async_remote_copy(
        src_ref=gathered.at[pl.ds(0, cols - 1)], dst_ref=gathered.at[pl.ds(0, cols - 1)],
        send_sem=col_send, recv_sem=col_recv, device_id=up, device_id_type=MESH,
    )
    sends.append(col_every)
    gathered[col] = sysl_ref[...]

    def place(block_of):
        def one(i, carry):
            blocks = [block_of(i, k) for k in range(8)]
            at = pl.multiple_of(i * PAD, PAD)
            for s in range(ROWS + 2):
                value = mask_ref[(i * 8) * (ROWS + 2) + s] * blocks[0]
                for k in range(1, 8):
                    value += mask_ref[(i * 8 + k) * (ROWS + 2) + s] * blocks[k]
                dense[pl.ds(at, BLK), s * PAD : s * PAD + BLK] = value
            return carry

        lax.fori_loop(0, ROWS, one, 0)

    def padded(block):
        wide = jnp.concatenate([block, jnp.zeros((BLK, PAD - BLK), F32)], axis=1)
        return jnp.concatenate([wide, jnp.zeros((PAD - BLK, PAD), F32)], axis=0)

    dense[...] = jnp.zeros_like(dense)
    place(lambda i, k: fac_ref[i, k])

    for i in range(ROWS):
        inverse = padded(dinv_ref[i])
        width = RIM + i * PAD
        given = dense[i * PAD : (i + 1) * PAD, :width]
        scaled = many(split(inverse), split(given))
        edge = scaled[:, :RIM]
        if i > 0:
            step = many(
                split(scaled[:, RIM:]), (xh[: i * PAD, :width], xl[: i * PAD, :width])
            )
            edge = edge - step[:, :RIM]
            body = [edge, -step[:, RIM:], inverse]
        else:
            body = [edge, inverse]
        if i < ROWS - 1:
            body.append(jnp.zeros((PAD, WIDE - (i + 1) * PAD), F32))
        high, low = split(jnp.concatenate(body, axis=1))
        xh[i * PAD : (i + 1) * PAD, :] = high
        xl[i * PAD : (i + 1) * PAD, :] = low
        if i >= ROWS - 2:
            at = (i - ROWS + 2) * BLK
            abuf[inner, at : at + BLK, :] = -edge[:BLK, :]

    a_every = spread(
        abuf, inner, [inner_peer(t) for t in range(1, span)], span - 1, a_send, a_recv
    )

    col_every.wait_recv()
    place(lambda i, k: gathered[k // share, i, k % share])
    for i in range(ROWS):
        high, low = split(dense[i * PAD : (i + 1) * PAD, :])
        lh[i * PAD : (i + 1) * PAD, :] = high
        ll[i * PAD : (i + 1) * PAD, :] = low
        high, low = split(padded(sysd_ref[i]))
        dh[i] = high
        dl[i] = low

    def spread_rows(value):
        gap = jnp.zeros((PAD - BLK, RIM), F32)
        return jnp.concatenate([value[:BLK], gap, value[BLK:], gap], axis=0)

    r_iota = lax.broadcasted_iota(jnp.int32, (RIM, RIM), 0)
    c_iota = lax.broadcasted_iota(jnp.int32, (RIM, RIM), 1)
    eye = jnp.where((r_iota == c_iota) & (c_iota % PAD < BLK), 1.0, 0.0).astype(F32)

    def put(refs, s, value):
        high, low = split(value)
        refs[0][s] = high
        refs[1][s] = low

    def get(refs, s):
        return refs[0][s], refs[1][s]

    a_refs, m_refs, r_refs, n_refs, p_refs = (ah, al), (mh, ml), (rh, rl), (nh, nl), (ph, pq)
    m2_refs, n2_refs = (m2h, m2l), (n2h, n2l)

    def flag(condition):
        return jnp.where(condition, 1.0, 0.0).astype(F32)

    a_every.wait_recv()
    for s in range(span):
        put(a_refs, s, spread_rows(abuf[s]))
    put(m_refs, span - 1, jnp.zeros((RIM, RIM), F32))
    put(r_refs, span - 1, eye)
    put(n_refs, 0, jnp.zeros((RIM, RIM), F32))
    put(p_refs, 0, eye)

    def chain(t, carry):
        s = span - 1 - t
        right = get(a_refs, s)
        put(m_refs, s - 1, many(get(m_refs, s), right) + flag(s == inner) * eye)
        put(r_refs, s - 1, many(get(r_refs, s), right))
        left = get(a_refs, t)
        put(n_refs, t + 1, many(left, get(n_refs, t)) + flag(t == inner) * eye)
        put(p_refs, t + 1, many(left, get(p_refs, t)))
        return carry

    lax.fori_loop(0, span - 1, chain, 0)
    across = many(get(a_refs, span - 1), get(p_refs, span - 1))
    bbuf[outer, :BLK, :] = across[:BLK]
    bbuf[outer, BLK:, :] = across[PAD : PAD + BLK]
    b_every = spread(
        bbuf, outer, [outer_peer(t) for t in range(1, spans)], spans - 1, b_send, b_recv
    )

    lane = lax.broadcasted_iota(jnp.int32, (columns, RIM), 1)

    def with_sum(value, sums):
        return jnp.where(lane == BLK, sums, jnp.where(lane % PAD < BLK, value, 0.0))

    def lane_sum(value):
        return jnp.sum(value, axis=1, keepdims=True)

    def exchange(phase, value, level):
        buf = ex.at[phase]
        if level == 0:
            buf[inner] = value
            peers, slot, count = [inner_peer(t) for t in range(1, span)], inner, span - 1
        else:
            buf[outer] = value
            peers, slot, count = [outer_peer(t) for t in range(1, spans)], outer, spans - 1
        return spread(buf, slot, peers, count, ex_send.at[phase], ex_recv.at[phase])

    def collect(phase, count, refs, nt):
        value = jnp.zeros((columns, RIM), F32)
        for s in range(count):
            value += few(stacked(ex[phase, s]), *get(refs, s), nt)
        return value

    def sums_of(phase, count):
        value = ex[phase, 0]
        for s in range(1, count):
            value += ex[phase, s]
        return lane_sum(jnp.where(lane == BLK, value, 0.0))

    tail = WIDE - RIM

    def forward_first(phase, source, sums):
        vs = stacked(source)
        rim = few(vs, xh[tail:, RIM:], xl[tail:, RIM:], True)
        wait = exchange(phase, with_sum(rim, sums), 0)
        parts = []
        for i in range(3):
            a, b = i * RIM, (i + 1) * RIM
            parts.append(few(vs[:, :b], xh[a:b, RIM : RIM + b], xl[a:b, RIM : RIM + b], True))
        local = jnp.concatenate(parts + [rim], axis=1)
        wait.wait_recv()
        value = collect(phase, span, r_refs, True)
        wait = exchange(phase + 1, with_sum(value, sums_of(phase, span)), 1)
        near = collect(phase, span, m_refs, True)
        return local, near, wait

    def forward_last(phase, local, near, wait):
        wait.wait_recv()
        entering = near + collect(phase + 1, spans, m2_refs, True)
        moved = few(stacked(entering), xh[:, :RIM], xl[:, :RIM], True)
        return local - moved, sums_of(phase + 1, spans)

    def backward(phase, source):
        vs = stacked(source)
        rim = few(vs, xh[:, :RIM], xl[:, :RIM], False)
        wait = exchange(phase, with_sum(rim, lane_sum(source * source)), 0)
        parts = []
        for i in range(4):
            a, b = i * RIM, (i + 1) * RIM
            parts.append(
                few(vs[:, a:], xh[a:, RIM + a : RIM + b], xl[a:, RIM + a : RIM + b], False)
            )
        local = jnp.concatenate(parts, axis=1)
        wait.wait_recv()
        value = collect(phase, span, p_refs, False)
        wait = exchange(phase + 1, with_sum(value, sums_of(phase, span)), 1)
        near = collect(phase, span, n_refs, False)
        wait.wait_recv()
        entering = near + collect(phase + 1, spans, n2_refs, False)
        moved = few(stacked(entering), xh[tail:, RIM:], xl[tail:, RIM:], False)
        return local - moved, sums_of(phase + 1, spans)

    def system_times(step, vector):
        vs = stacked(vector)
        falling = few(vs, lh[:, :RIM], ll[:, :RIM], False)
        last = vector[:, tail:] + few(
            vs[:, tail:], lh[tail:, RIM + tail :], ll[tail:, RIM + tail :], False
        )
        nbs[step, 0] = falling
        nbs[step, 1] = last
        copies = []
        for way, peer in ((0, down), (1, up)):
            copy = pltpu.make_async_remote_copy(
                src_ref=nbs.at[step, way], dst_ref=nbr.at[step, way],
                send_sem=nb_send.at[step, way], recv_sem=nb_recv.at[step, way],
                device_id=peer, device_id_type=MESH,
            )
            copy.start()
            copies.append(copy)
            sends.append(copy)
        parts = []
        for i in range(3):
            a, b = i * RIM, (i + 1) * RIM
            parts.append(
                vector[:, a:b]
                + few(vs[:, a:], lh[a:, RIM + a : RIM + b], ll[a:, RIM + a : RIM + b], False)
            )
        upper = jnp.concatenate(parts + [last], axis=1)
        us = stacked(upper)
        parts = []
        for i in range(4):
            a, b = i * RIM, (i + 1) * RIM
            parts.append(few(us[:, :b], lh[a:b, RIM : RIM + b], ll[a:b, RIM : RIM + b], True))
        diagonal = [
            few(vs[:, i * PAD : (i + 1) * PAD], dh[i], dl[i], False) for i in range(ROWS)
        ]
        image = upper + jnp.concatenate(parts, axis=1) + jnp.concatenate(diagonal, axis=1)
        copies[0].wait_recv()
        coming = nbr[step, 0] * flag(row < total - 1)
        corner = coming + few(
            stacked(coming), lh[tail:, RIM + tail :], ll[tail:, RIM + tail :], True
        )
        copies[1].wait_recv()
        before = (nbr[step, 1] + falling) * flag(row > 0)
        image = image + few(stacked(before), lh[:, :RIM], ll[:, :RIM], True)
        return jnp.concatenate([image[:, :tail], image[:, tail:] + corner], axis=1)

    residual = rhs_ref[...]
    state = forward_first(0, residual, jnp.zeros((columns, 1), F32))

    b_every.wait_recv()
    for s in range(spans):
        put(a_refs, s, spread_rows(bbuf[s]))
    mine_p = ph[inner].astype(F32) + pq[inner].astype(F32)
    mine_r = rh[inner].astype(F32) + rl[inner].astype(F32)
    put(m2_refs, spans - 1, jnp.zeros((RIM, RIM), F32))
    put(n2_refs, 0, jnp.zeros((RIM, RIM), F32))

    def outer_chain(t, carry):
        s = spans - 1 - t
        put(m2_refs, s - 1, many(get(m2_refs, s), get(a_refs, s)) + flag(s == outer) * mine_p)
        put(n2_refs, t + 1, many(get(a_refs, t), get(n2_refs, t)) + flag(t == outer) * mine_r)
        return carry

    lax.fori_loop(0, spans - 1, outer_chain, 0)

    solved, _ = forward_last(0, *state)
    direction, energy = backward(2, solved)
    answer = jnp.zeros_like(residual)
    for step in range(ITERS):
        phase = 4 * (step + 1)
        image = system_times(step, direction)
        state = forward_first(phase, image, lane_sum(direction * image))
        change, curvature = forward_last(phase, *state)
        alpha = energy / curvature
        answer = answer + alpha * direction
        residual = residual - alpha * image
        solved = solved - alpha * change
        precond, energy_next = backward(phase + 2, solved)
        direction = precond + (energy_next / energy) * direction
        energy = energy_next

    sol_ref[...] = answer
    res_ref[...] = residual
    dir_ref[...] = direction
    for copy in sends:
        copy.wait_send()


def per_device(
    spans, cols, rhs, system_lower, system_diag, factor_lower, diag_inverse, neighbours, counts
):
    rows, width, columns = rhs.shape
    places = neighbours - lax.axis_index("row") * rows + 2
    live = jnp.arange(8, dtype=jnp.int32)[None, :] < counts[:, None]
    mask = (places[:, :, None] == jnp.arange(rows + 2, dtype=jnp.int32)) & live[:, :, None]
    mask = mask.astype(F32).reshape(-1)
    turned = jnp.pad(jnp.transpose(rhs, (2, 0, 1)), ((0, 0), (0, 0), (0, PAD - width)))
    turned = turned.reshape(columns, WIDE)
    vmem = pl.BlockSpec(memory_space=pltpu.VMEM)
    phases = 4 * (ITERS + 1)
    half = lambda: pltpu.VMEM((GROUP, RIM, RIM), BF16)
    most = max(GROUP, spans)
    tall = lambda: pltpu.VMEM((most, RIM, RIM), BF16)
    dma = pltpu.SemaphoreType.DMA
    outs = pl.pallas_call(
        functools.partial(kernel, GROUP, spans, cols),
        out_shape=[jax.ShapeDtypeStruct((columns, WIDE), F32)] * 3,
        in_specs=[pl.BlockSpec(memory_space=pltpu.SMEM)] + [vmem] * 5,
        out_specs=[vmem] * 3,
        scratch_shapes=[
            pltpu.VMEM((WIDE, RIM + WIDE), F32),
            pltpu.VMEM((WIDE, RIM + WIDE), BF16),
            pltpu.VMEM((WIDE, RIM + WIDE), BF16),
            pltpu.VMEM((WIDE, RIM + WIDE), BF16),
            pltpu.VMEM((WIDE, RIM + WIDE), BF16),
            pltpu.VMEM((ROWS, PAD, PAD), BF16),
            pltpu.VMEM((ROWS, PAD, PAD), BF16),
            pltpu.VMEM((cols,) + system_lower.shape, F32),
            pltpu.VMEM((GROUP, 2 * BLK, RIM), F32),
            pltpu.VMEM((spans, 2 * BLK, RIM), F32),
            tall(), tall(),
            half(), half(), half(), half(), half(), half(), half(), half(),
            tall(), tall(), tall(), tall(),
            pltpu.VMEM((phases, most, columns, RIM), F32),
            pltpu.VMEM((ITERS, 2, columns, RIM), F32),
            pltpu.VMEM((ITERS, 2, columns, RIM), F32),
            dma, dma, dma, dma, dma, dma,
            dma((phases,)), dma((phases,)), dma((ITERS, 2)), dma((ITERS, 2)),
        ],
        compiler_params=pltpu.CompilerParams(
            collective_id=0, has_side_effects=True, vmem_limit_bytes=60 * 1024 * 1024
        ),
    )(mask, turned, system_lower, system_diag, factor_lower, diag_inverse)

    def back(value):
        return jnp.transpose(value.reshape(columns, rows, PAD)[:, :, :width], (1, 2, 0))

    return tuple(back(value) for value in outs)


def solution(mesh):
    in_specs = (
        P("row", None, "col"),
        P("row", "col", None, None),
        P("row", None, None),
        P("row", None, None, None),
        P("row", None, None),
        P("row", None),
        P("row"),
    )
    out_specs = (P("row", None, "col"), P("row", None, "col"), P("row", None, "col"))
    return jax.shard_map(
        functools.partial(per_device, mesh.shape["row"] // GROUP, mesh.shape["col"]),
        mesh=mesh, in_specs=in_specs, out_specs=out_specs, check_vma=False,
    )
```

```python
import functools

import jax
import jax.numpy as jnp
from jax import lax
from jax.experimental import pallas as pl
from jax.experimental.pallas import tpu as pltpu
from jax.sharding import PartitionSpec as P

ITERS = 2
GROUP = 8
BLK = 72
ROWS = 8
PAD = 128
WIDE = ROWS * PAD
RIM = 2 * PAD
PACKED = BLK + 16
F32 = jnp.float32
BF16 = jnp.bfloat16
MESH = pl.DeviceIdType.MESH


def split(x):
    high = x.astype(BF16)
    return high, (x - high.astype(F32)).astype(BF16)


def dot(a, b, nt):
    return lax.dot_general(
        a, b, (((1,), (1 if nt else 0,)), ((), ())), preferred_element_type=F32
    )


def stacked(v):
    high, low = split(v)
    return jnp.concatenate([high, low], axis=0)


def few(vs, high, low, nt):
    rows = vs.shape[0] // 2
    both = dot(vs, high, nt)
    return both[:rows] + both[rows:] + dot(vs[:rows], low, nt)


def many(a, b, nt=False):
    return dot(a[0], b[0], nt) + (dot(a[0], b[1], nt) + dot(a[1], b[0], nt))


def nearest(count):
    return sorted(range(1, count), key=lambda t: min(t, count - t))


def pack(half):
    lane = lax.broadcasted_iota(jnp.int32, (BLK, PAD), 1)
    turned = pltpu.roll(half[:, PAD:], BLK, 1)
    top = jnp.where(lane < BLK, half[:, :PAD], turned)
    rest = jnp.where(lane < 16, turned, 0.0)
    first = rest[:8]
    for g in range(1, 8):
        first += pltpu.roll(rest[8 * g : 8 * g + 8], 16 * g, 1)
    return jnp.concatenate([top, first, rest[64:]], axis=0)


def unpack(packed):
    lane = lax.broadcasted_iota(jnp.int32, (BLK, PAD), 1)
    top, first, last = packed[:BLK], packed[BLK : BLK + 8], packed[BLK + 8 :]
    edge = PAD - BLK
    rest = [pltpu.roll(first, (edge - 16 * g) % PAD, 1) for g in range(8)]
    rest = jnp.concatenate(rest + [pltpu.roll(last, edge, 1)], axis=0)
    right = jnp.where(lane < edge, pltpu.roll(top, edge, 1), jnp.where(lane < BLK, rest, 0.0))
    left = jnp.where(lane < BLK, top, 0.0)
    value = jnp.concatenate([left, right], axis=1)
    return jnp.concatenate([value, jnp.zeros((PAD - BLK, RIM), F32)], axis=0)


def kernel(
    span, spans, cols, neighbours_ref, counts_ref, rhs_ref, sysl_ref, sysd_ref, fac_ref, dinv_ref,
    sol_ref, res_ref, dir_ref,
    dense, xh, xl, lh, ll, dh, dl, gathered, abuf, bbuf, ah, al,
    mh, ml, rh, rl, nh, nl, ph, pq, m2h, m2l, n2h, n2l, ex, nbs, nbr,
    col_send, col_recv, a_send, a_recv, b_send, b_recv, ex_send, ex_recv, nb_send, nb_recv,
):
    row, col = lax.axis_index("row"), lax.axis_index("col")
    total = span * spans
    outer, inner = row // span, row % span
    share = sysl_ref.shape[1]
    columns = rhs_ref.shape[1]
    chips = span // 2
    chip, core = inner // 2, inner % 2

    def at_inner(x, c):
        return ((chip + x + chips) % chips) * 2 + (core + c + 2) % 2

    def at_outer(t):
        return (outer + t + spans) % spans

    def inner_peer(x, c):
        return (outer * span + at_inner(x, c), col)

    def outer_peer(t):
        return (at_outer(t) * span + inner, col)

    inner_steps = [(x, c) for x in [0] + nearest(chips) for c in range(2)][1:]
    outer_steps = nearest(spans)
    up, down = ((row + 1) % total, col), ((row + total - 1) % total, col)
    sibling = inner_peer(0, 1)

    barrier = pltpu.get_barrier_semaphore()
    greeted = (
        [inner_peer(*t) for t in inner_steps]
        + [outer_peer(t) for t in outer_steps]
        + [(row, (col + t) % cols) for t in range(1, cols)]
        + [up, down]
    )
    for peer in greeted:
        pl.semaphore_signal(barrier, inc=1, device_id=peer, device_id_type=MESH)

    sends = []

    def remote(source, target, send_sem, recv_sem, peer):
        return pltpu.make_async_remote_copy(
            src_ref=source, dst_ref=target, send_sem=send_sem, recv_sem=recv_sem,
            device_id=peer, device_id_type=MESH,
        )

    def place(block_of):
        def one(i, carry):
            blocks = [block_of(i, k) for k in range(8)]
            at = pl.multiple_of(i * PAD, PAD)
            places = [
                jnp.where(k < counts_ref[i], neighbours_ref[i, k] - row * ROWS + 2, -1)
                for k in range(8)
            ]
            for s in range(ROWS + 2):
                value = jnp.where(places[0] == s, 1.0, 0.0) * blocks[0]
                for k in range(1, 8):
                    value += jnp.where(places[k] == s, 1.0, 0.0) * blocks[k]
                dense[pl.ds(at, BLK), s * PAD : s * PAD + BLK] = value
            return carry

        lax.fori_loop(0, ROWS, one, 0)

    def padded(block):
        wide = jnp.concatenate([block, jnp.zeros((BLK, PAD - BLK), F32)], axis=1)
        return jnp.concatenate([wide, jnp.zeros((PAD - BLK, PAD), F32)], axis=0)

    dense[...] = jnp.zeros_like(dense)
    place(lambda i, k: fac_ref[i, k])

    for i in range(ROWS):
        inverse = padded(dinv_ref[i])
        width = RIM + i * PAD
        given = dense[i * PAD : (i + 1) * PAD, :width]
        scaled = many(split(inverse), split(given))
        edge = scaled[:, :RIM]
        if i > 0:
            step = many(
                split(scaled[:, RIM:]), (xh[: i * PAD, :width], xl[: i * PAD, :width])
            )
            edge = edge - step[:, :RIM]
            body = [edge, -step[:, RIM:], inverse]
        else:
            body = [edge, inverse]
        if i < ROWS - 1:
            body.append(jnp.zeros((PAD, WIDE - (i + 1) * PAD), F32))
        high, low = split(jnp.concatenate(body, axis=1))
        xh[i * PAD : (i + 1) * PAD, :] = high
        xl[i * PAD : (i + 1) * PAD, :] = low
        if i >= ROWS - 2:
            abuf[inner, i - ROWS + 2] = pack(-edge[:BLK, :])

    pl.semaphore_wait(barrier, len(greeted))

    def hand(buf, slot, n, send, recv, peer):
        copy = remote(buf.at[slot], buf.at[slot], send.at[n], recv.at[n], peer)
        copy.start()
        sends.append(copy)

    def awaited(buf, slot, n, send, recv):
        remote(buf.at[slot], buf.at[slot], send.at[n], recv.at[n], sibling).wait_recv()

    for x in reversed(nearest(chips)):
        hand(abuf, inner, x, a_send, a_recv, inner_peer(x, 0))
    hand(abuf, inner, 0, a_send, a_recv, sibling)

    lane = lax.broadcasted_iota(jnp.int32, (columns, RIM), 1)

    def with_sum(value, sums):
        return jnp.where(lane == BLK, sums, jnp.where(lane % PAD < BLK, value, 0.0))

    def lane_sum(value):
        return jnp.sum(value, axis=1, keepdims=True)

    def get(refs, s):
        return refs[0][s], refs[1][s]

    def exchange(phase, value, level):
        buf = ex.at[phase]
        mine, steps, peer_of, count = (
            (inner, inner_steps, lambda t: inner_peer(*t), span)
            if level == 0
            else (outer, outer_steps, outer_peer, spans)
        )
        buf[mine] = value
        coming = []
        for n, t in reversed(list(enumerate(steps))):
            sems = ex_send.at[phase], ex_recv.at[phase, n]
            remote(buf.at[mine], buf.at[mine], *sems, peer_of(t)).start()
            origin = at_inner(-t[0], -t[1]) if level == 0 else at_outer(-t)
            coming.append((origin, remote(buf.at[origin], buf.at[origin], *sems, sibling)))
        every = buf.at[pl.ds(0, count - 1)]
        sends.append(remote(every, every, ex_send.at[phase], ex_recv.at[phase, 0], sibling))
        return phase, mine, value, coming[::-1]

    def collect(exchanged, refs, nt):
        phase, mine, value, coming = exchanged
        result = few(stacked(value), *get(refs, mine), nt)
        for origin, copy in coming:
            copy.wait_recv()
            arrived = ex[phase, origin]
            value = value + arrived
            result += few(stacked(arrived), *get(refs, origin), nt)
        return result, lane_sum(jnp.where(lane == BLK, value, 0.0))

    def again(exchanged, refs, nt):
        phase, mine, value, coming = exchanged
        result = few(stacked(value), *get(refs, mine), nt)
        for origin, _ in coming:
            result += few(stacked(ex[phase, origin]), *get(refs, origin), nt)
        return result

    tail = WIDE - RIM

    def forward_local(phase, source, sums):
        vs = stacked(source)
        rim = few(vs, xh[tail:, RIM:], xl[tail:, RIM:], True)
        near = exchange(phase, with_sum(rim, sums), 0)
        parts = []
        for i in range(3):
            a, b = i * RIM, (i + 1) * RIM
            parts.append(few(vs[:, :b], xh[a:b, RIM : RIM + b], xl[a:b, RIM : RIM + b], True))
        return near, jnp.concatenate(parts + [rim], axis=1)

    def across_spans(phase, near, first, second, nt):
        value, sums = collect(near, first, nt)
        far = exchange(phase, with_sum(value, sums), 1)
        return far, again(near, second, nt)

    def forward_last(far, local, entering):
        value, sums = collect(far, m2_refs, True)
        moved = few(stacked(entering + value), xh[:, :RIM], xl[:, :RIM], True)
        return local - moved, sums

    def backward(phase, source, beside=None):
        vs = stacked(source)
        rim = few(vs, xh[:, :RIM], xl[:, :RIM], False)
        near = exchange(phase, with_sum(rim, lane_sum(source * source)), 0)
        parts = []
        for i in range(4):
            a, b = i * RIM, (i + 1) * RIM
            parts.append(
                few(vs[:, a:], xh[a:, RIM + a : RIM + b], xl[a:, RIM + a : RIM + b], False)
            )
        local = jnp.concatenate(parts, axis=1)
        far, entering = across_spans(phase + 1, near, p_refs, n_refs, False)
        if beside is not None:
            beside()
        value, sums = collect(far, n2_refs, False)
        moved = few(stacked(entering + value), xh[tail:, RIM:], xl[tail:, RIM:], False)
        return local - moved, sums

    def system_times(step, vector):
        vs = stacked(vector)
        falling = few(vs, lh[:, :RIM], ll[:, :RIM], False)
        last = vector[:, tail:] + few(
            vs[:, tail:], lh[tail:, RIM + tail :], ll[tail:, RIM + tail :], False
        )
        nbs[step, 0] = falling
        nbs[step, 1] = last
        copies = []
        for way, peer in ((0, down), (1, up)):
            copy = remote(
                nbs.at[step, way], nbr.at[step, way],
                nb_send.at[step, way], nb_recv.at[step, way], peer,
            )
            copy.start()
            copies.append(copy)
            sends.append(copy)
        parts = []
        for i in range(3):
            a, b = i * RIM, (i + 1) * RIM
            parts.append(
                vector[:, a:b]
                + few(vs[:, a:], lh[a:, RIM + a : RIM + b], ll[a:, RIM + a : RIM + b], False)
            )
        upper = jnp.concatenate(parts + [last], axis=1)
        us = stacked(upper)
        parts = []
        for i in range(4):
            a, b = i * RIM, (i + 1) * RIM
            parts.append(few(us[:, :b], lh[a:b, RIM : RIM + b], ll[a:b, RIM : RIM + b], True))
        diagonal = [
            few(vs[:, i * PAD : (i + 1) * PAD], dh[i], dl[i], False) for i in range(ROWS)
        ]
        image = upper + jnp.concatenate(parts, axis=1) + jnp.concatenate(diagonal, axis=1)
        copies[0].wait_recv()
        coming = nbr[step, 0] * flag(row < total - 1)
        corner = coming + few(
            stacked(coming), lh[tail:, RIM + tail :], ll[tail:, RIM + tail :], True
        )
        copies[1].wait_recv()
        before = (nbr[step, 1] + falling) * flag(row > 0)
        image = image + few(stacked(before), lh[:, :RIM], ll[:, :RIM], True)
        return jnp.concatenate([image[:, :tail], image[:, tail:] + corner], axis=1)

    gap = jnp.zeros((columns, PAD - BLK), F32)
    residual = jnp.concatenate(
        [part for i in range(ROWS) for part in (rhs_ref[i], gap)], axis=1
    )
    near, local = forward_local(0, residual, jnp.zeros((columns, 1), F32))

    for t in range(1, cols):
        remote(
            sysl_ref, gathered.at[col], col_send, col_recv, (row, (col + t) % cols)
        ).start()
    others = gathered.at[pl.ds(0, cols - 1)]
    col_every = remote(others, others, col_send, col_recv, up)
    sends.append(col_every)
    gathered[col] = sysl_ref[...]

    def place_system():
        col_every.wait_recv()
        place(lambda i, k: gathered[k // share, i, k % share])
        for i in range(ROWS):
            high, low = split(dense[i * PAD : (i + 1) * PAD, :])
            lh[i * PAD : (i + 1) * PAD, :] = high
            ll[i * PAD : (i + 1) * PAD, :] = low
            high, low = split(padded(sysd_ref[i]))
            dh[i] = high
            dl[i] = low

    r_iota = lax.broadcasted_iota(jnp.int32, (RIM, RIM), 0)
    c_iota = lax.broadcasted_iota(jnp.int32, (RIM, RIM), 1)
    eye = jnp.where((r_iota == c_iota) & (c_iota % PAD < BLK), 1.0, 0.0).astype(F32)

    def put(refs, s, value):
        high, low = split(value)
        refs[0][s] = high
        refs[1][s] = low

    a_refs, m_refs, r_refs, n_refs, p_refs = (ah, al), (mh, ml), (rh, rl), (nh, nl), (ph, pq)
    m2_refs, n2_refs = (m2h, m2l), (n2h, n2l)

    def flag(condition):
        return jnp.where(condition, 1.0, 0.0).astype(F32)

    def unpack_all(buf, s, carry):
        put(a_refs, s, jnp.concatenate([unpack(buf[s, 0]), unpack(buf[s, 1])], axis=0))
        return carry

    for x in nearest(chips):
        origin = at_inner(-x, 0)
        awaited(abuf, origin, x, a_send, a_recv)
        hand(abuf, origin, chips + x, a_send, a_recv, sibling)
    awaited(abuf, at_inner(0, 1), 0, a_send, a_recv)
    for x in nearest(chips):
        awaited(abuf, at_inner(-x, 1), chips + x, a_send, a_recv)
    lax.fori_loop(0, span, functools.partial(unpack_all, abuf), 0)
    put(m_refs, span - 1, jnp.zeros((RIM, RIM), F32))
    put(r_refs, span - 1, eye)
    put(n_refs, 0, jnp.zeros((RIM, RIM), F32))
    put(p_refs, 0, eye)

    def chain(t, carry):
        s = span - 1 - t
        right = get(a_refs, s)
        put(m_refs, s - 1, many(get(m_refs, s), right) + flag(s == inner) * eye)
        put(r_refs, s - 1, many(get(r_refs, s), right))
        left = get(a_refs, t)
        put(n_refs, t + 1, many(left, get(n_refs, t)) + flag(t == inner) * eye)
        put(p_refs, t + 1, many(left, get(p_refs, t)))
        return carry

    lax.fori_loop(0, span - 1, chain, 0)
    across = many(get(a_refs, span - 1), get(p_refs, span - 1))
    bbuf[outer, 0] = pack(across[:BLK])
    bbuf[outer, 1] = pack(across[PAD : PAD + BLK])
    for t in reversed(outer_steps):
        hand(bbuf, (outer, core), t, b_send, b_recv, outer_peer(t))
    far, entering = across_spans(1, near, r_refs, m_refs, True)

    for t in outer_steps:
        origin = at_outer(-t)
        awaited(bbuf, (origin, core), t, b_send, b_recv)
        hand(bbuf, (origin, core), spans + t, b_send, b_recv, sibling)
    for t in outer_steps:
        awaited(bbuf, (at_outer(-t), 1 - core), spans + t, b_send, b_recv)
    lax.fori_loop(0, spans, functools.partial(unpack_all, bbuf), 0)
    mine_p = ph[inner].astype(F32) + pq[inner].astype(F32)
    mine_r = rh[inner].astype(F32) + rl[inner].astype(F32)
    put(m2_refs, spans - 1, jnp.zeros((RIM, RIM), F32))
    put(n2_refs, 0, jnp.zeros((RIM, RIM), F32))

    def outer_chain(t, carry):
        s = spans - 1 - t
        put(m2_refs, s - 1, many(get(m2_refs, s), get(a_refs, s)) + flag(s == outer) * mine_p)
        put(n2_refs, t + 1, many(get(a_refs, t), get(n2_refs, t)) + flag(t == outer) * mine_r)
        return carry

    lax.fori_loop(0, spans - 1, outer_chain, 0)

    solved, _ = forward_last(far, local, entering)
    direction, energy = backward(2, solved, place_system)
    answer = jnp.zeros_like(residual)
    for step in range(ITERS):
        phase = 4 * (step + 1)
        image = system_times(step, direction)
        near, local = forward_local(phase, image, lane_sum(direction * image))
        far, entering = across_spans(phase + 1, near, r_refs, m_refs, True)
        change, curvature = forward_last(far, local, entering)
        alpha = energy / curvature
        answer = answer + alpha * direction
        residual = residual - alpha * image
        solved = solved - alpha * change
        precond, energy_next = backward(phase + 2, solved)
        direction = precond + (energy_next / energy) * direction
        energy = energy_next

    for i in range(ROWS):
        lanes = slice(i * PAD, i * PAD + BLK)
        sol_ref[i] = answer[:, lanes]
        res_ref[i] = residual[:, lanes]
        dir_ref[i] = direction[:, lanes]
    for copy in sends:
        copy.wait_send()


def per_device(
    spans, cols, rhs, system_lower, system_diag, factor_lower, diag_inverse, neighbours, counts
):
    rows, width, columns = rhs.shape
    vmem = pl.BlockSpec(memory_space=pltpu.VMEM)
    phases = 4 * (ITERS + 1)
    half = lambda: pltpu.VMEM((GROUP, RIM, RIM), BF16)
    most = max(GROUP, spans)
    tall = lambda: pltpu.VMEM((most, RIM, RIM), BF16)
    dma = pltpu.SemaphoreType.DMA
    outs = pl.pallas_call(
        functools.partial(kernel, GROUP, spans, cols),
        out_shape=[jax.ShapeDtypeStruct((rows, columns, width), F32)] * 3,
        in_specs=[pl.BlockSpec(memory_space=pltpu.SMEM)] * 2 + [vmem] * 5,
        out_specs=[vmem] * 3,
        scratch_shapes=[
            pltpu.VMEM((WIDE, RIM + WIDE), F32),
            pltpu.VMEM((WIDE, RIM + WIDE), BF16),
            pltpu.VMEM((WIDE, RIM + WIDE), BF16),
            pltpu.VMEM((WIDE, RIM + WIDE), BF16),
            pltpu.VMEM((WIDE, RIM + WIDE), BF16),
            pltpu.VMEM((ROWS, PAD, PAD), BF16),
            pltpu.VMEM((ROWS, PAD, PAD), BF16),
            pltpu.VMEM((cols,) + system_lower.shape, F32),
            pltpu.VMEM((GROUP, 2, PACKED, PAD), F32),
            pltpu.VMEM((spans, 2, PACKED, PAD), F32),
            tall(), tall(),
            half(), half(), half(), half(), half(), half(), half(), half(),
            tall(), tall(), tall(), tall(),
            pltpu.VMEM((phases, most, columns, RIM), F32),
            pltpu.VMEM((ITERS, 2, columns, RIM), F32),
            pltpu.VMEM((ITERS, 2, columns, RIM), F32),
            dma, dma, dma((GROUP,)), dma((GROUP,)), dma((2 * spans,)), dma((2 * spans,)),
            dma((phases,)), dma((phases, most - 1)), dma((ITERS, 2)), dma((ITERS, 2)),
        ],
        compiler_params=pltpu.CompilerParams(
            collective_id=0, has_side_effects=True, vmem_limit_bytes=60 * 1024 * 1024
        ),
    )(
        neighbours, counts, jnp.transpose(rhs, (0, 2, 1)), system_lower, system_diag,
        factor_lower, diag_inverse,
    )
    return tuple(jnp.transpose(value, (0, 2, 1)) for value in outs)


def solution(mesh):
    in_specs = (
        P("row", None, "col"),
        P("row", "col", None, None),
        P("row", None, None),
        P("row", None, None, None),
        P("row", None, None),
        P("row", None),
        P("row"),
    )
    out_specs = (P("row", None, "col"), P("row", None, "col"), P("row", None, "col"))
    return jax.shard_map(
        functools.partial(per_device, mesh.shape["row"] // GROUP, mesh.shape["col"]),
        mesh=mesh, in_specs=in_specs, out_specs=out_specs, check_vma=False,
    )
```

```python
import functools

import jax
import jax.numpy as jnp
from jax import lax
from jax.experimental import pallas as pl
from jax.experimental.pallas import tpu as pltpu
from jax.sharding import PartitionSpec as P

ITERS = 2
GROUP = 8
BLK = 72
ROWS = 8
PAD = 128
WIDE = ROWS * PAD
RIM = 2 * PAD
PACKED = BLK + 16
F32 = jnp.float32
BF16 = jnp.bfloat16
MESH = pl.DeviceIdType.MESH


def split(x):
    high = x.astype(BF16)
    return high, (x - high.astype(F32)).astype(BF16)


def dot(a, b, nt):
    return lax.dot_general(
        a, b, (((1,), (1 if nt else 0,)), ((), ())), preferred_element_type=F32
    )


def stacked(v):
    high, low = split(v)
    return jnp.concatenate([high, low], axis=0)


def few(vs, high, low, nt):
    rows = vs.shape[0] // 2
    both = dot(vs, high, nt)
    return both[:rows] + both[rows:] + dot(vs[:rows], low, nt)


def many(a, b, nt=False):
    return dot(a[0], b[0], nt) + (dot(a[0], b[1], nt) + dot(a[1], b[0], nt))


def nearest(count):
    return sorted(range(1, count), key=lambda t: min(t, count - t))


def pack(half):
    lane = lax.broadcasted_iota(jnp.int32, (BLK, PAD), 1)
    turned = pltpu.roll(half[:, PAD:], BLK, 1)
    top = jnp.where(lane < BLK, half[:, :PAD], turned)
    rest = jnp.where(lane < 16, turned, 0.0)
    first = rest[:8]
    for g in range(1, 8):
        first += pltpu.roll(rest[8 * g : 8 * g + 8], 16 * g, 1)
    return jnp.concatenate([top, first, rest[64:]], axis=0)


def unpack(packed):
    lane = lax.broadcasted_iota(jnp.int32, (BLK, PAD), 1)
    top, first, last = packed[:BLK], packed[BLK : BLK + 8], packed[BLK + 8 :]
    edge = PAD - BLK
    rest = [pltpu.roll(first, (edge - 16 * g) % PAD, 1) for g in range(8)]
    rest = jnp.concatenate(rest + [pltpu.roll(last, edge, 1)], axis=0)
    right = jnp.where(lane < edge, pltpu.roll(top, edge, 1), jnp.where(lane < BLK, rest, 0.0))
    left = jnp.where(lane < BLK, top, 0.0)
    value = jnp.concatenate([left, right], axis=1)
    return jnp.concatenate([value, jnp.zeros((PAD - BLK, RIM), F32)], axis=0)


def kernel(
    span, spans, cols, neighbours_ref, counts_ref, rhs_ref, sysl_ref, sysd_ref, fac_ref, dinv_ref,
    out_ref,
    dense, xh, xl, lh, ll, dh, dl, gathered, abuf, bbuf, ah, al,
    mh, ml, rh, rl, nh, nl, ph, pq, m2h, m2l, n2h, n2l, ex, nbs, nbr,
    own_sem, col_send, col_recv, a_send, a_recv, b_send, b_recv, ex_send, ex_recv, nb_send, nb_recv,
):
    row, col = lax.axis_index("row"), lax.axis_index("col")
    total = span * spans
    outer, inner = row // span, row % span
    share = sysl_ref.shape[1]
    columns = rhs_ref.shape[1]
    chips = span // 2
    chip, core = inner // 2, inner % 2

    def at_inner(x, c):
        return ((chip + x + chips) % chips) * 2 + (core + c + 2) % 2

    def at_outer(t):
        return (outer + t + spans) % spans

    def inner_peer(x, c):
        return (outer * span + at_inner(x, c), col)

    def outer_peer(t):
        return (at_outer(t) * span + inner, col)

    inner_steps = [(x, c) for x in [0] + nearest(chips) for c in range(2)][1:]
    outer_steps = nearest(spans)
    up, down = ((row + 1) % total, col), ((row + total - 1) % total, col)
    sibling = inner_peer(0, 1)

    barrier = pltpu.get_barrier_semaphore()
    greeted = (
        [inner_peer(*t) for t in inner_steps]
        + [outer_peer(t) for t in outer_steps]
        + [(row, (col + t) % cols) for t in range(1, cols)]
        + [up, down]
    )
    for peer in greeted:
        pl.semaphore_signal(barrier, inc=1, device_id=peer, device_id_type=MESH)

    sends = []

    def remote(source, target, send_sem, recv_sem, peer):
        return pltpu.make_async_remote_copy(
            src_ref=source, dst_ref=target, send_sem=send_sem, recv_sem=recv_sem,
            device_id=peer, device_id_type=MESH,
        )

    def place(block_of):
        def one(i, carry):
            blocks = [block_of(i, k) for k in range(8)]
            at = pl.multiple_of(i * PAD, PAD)
            places = [
                jnp.where(k < counts_ref[i], neighbours_ref[i, k] - row * ROWS + 2, -1)
                for k in range(8)
            ]
            for s in range(ROWS + 2):
                value = jnp.where(places[0] == s, 1.0, 0.0) * blocks[0]
                for k in range(1, 8):
                    value += jnp.where(places[k] == s, 1.0, 0.0) * blocks[k]
                dense[pl.ds(at, BLK), s * PAD : s * PAD + BLK] = value
            return carry

        lax.fori_loop(0, ROWS, one, 0)

    def padded(block):
        wide = jnp.concatenate([block, jnp.zeros((BLK, PAD - BLK), F32)], axis=1)
        return jnp.concatenate([wide, jnp.zeros((PAD - BLK, PAD), F32)], axis=0)

    dense[...] = jnp.zeros_like(dense)
    place(lambda i, k: fac_ref[i, k])

    inverses = [padded(dinv_ref[i]) for i in range(ROWS)]
    scaled = [
        many(split(inverses[i]), split(dense[i * PAD : (i + 1) * PAD, : RIM + i * PAD]))
        for i in range(ROWS)
    ]
    nothing = jnp.zeros((PAD, PAD), F32)
    for i in range(0, ROWS, 2):
        width = RIM + i * PAD
        first, second = scaled[i], scaled[i + 1][:, :width]
        taken = many(
            split(scaled[i + 1][:, width:]),
            split(jnp.concatenate([first, inverses[i]], axis=1)),
        )
        rows = jnp.concatenate([first, second - taken[:, :width]], axis=0)
        corner = jnp.concatenate(
            [
                jnp.concatenate([inverses[i], nothing], axis=1),
                jnp.concatenate([-taken[:, width:], inverses[i + 1]], axis=1),
            ],
            axis=0,
        )
        edge = rows[:, :RIM]
        if i > 0:
            step = many(split(rows[:, RIM:]), (xh[: i * PAD, :width], xl[: i * PAD, :width]))
            edge = edge - step[:, :RIM]
            body = [edge, -step[:, RIM:], corner]
        else:
            body = [edge, corner]
        if i < ROWS - 2:
            body.append(jnp.zeros((2 * PAD, WIDE - (i + 2) * PAD), F32))
        high, low = split(jnp.concatenate(body, axis=1))
        xh[i * PAD : (i + 2) * PAD, :] = high
        xl[i * PAD : (i + 2) * PAD, :] = low
    abuf[inner, 0] = pack(-edge[:BLK, :])
    abuf[inner, 1] = pack(-edge[PAD : PAD + BLK, :])

    pl.semaphore_wait(barrier, len(greeted))

    def hand(buf, slot, n, send, recv, peer):
        copy = remote(buf.at[slot], buf.at[slot], send.at[n], recv.at[n], peer)
        copy.start()
        sends.append(copy)

    def awaited(buf, slot, n, send, recv):
        remote(buf.at[slot], buf.at[slot], send.at[n], recv.at[n], sibling).wait_recv()

    for x in reversed(nearest(chips)):
        hand(abuf, inner, x, a_send, a_recv, inner_peer(x, 0))
    hand(abuf, inner, 0, a_send, a_recv, sibling)

    lane = lax.broadcasted_iota(jnp.int32, (columns, RIM), 1)

    def with_sum(value, sums):
        return jnp.where(lane == BLK, sums, jnp.where(lane % PAD < BLK, value, 0.0))

    def lane_sum(value):
        return jnp.sum(value, axis=1, keepdims=True)

    def get(refs, s):
        return refs[0][s], refs[1][s]

    def exchange(phase, value, level):
        buf = ex.at[phase]
        mine, steps, peer_of, count = (
            (inner, inner_steps, lambda t: inner_peer(*t), span)
            if level == 0
            else (outer, outer_steps, outer_peer, spans)
        )
        buf[mine] = value
        coming = []
        for n, t in reversed(list(enumerate(steps))):
            sems = ex_send.at[phase], ex_recv.at[phase, n]
            remote(buf.at[mine], buf.at[mine], *sems, peer_of(t)).start()
            origin = at_inner(-t[0], -t[1]) if level == 0 else at_outer(-t)
            coming.append((origin, remote(buf.at[origin], buf.at[origin], *sems, sibling)))
        every = buf.at[pl.ds(0, count - 1)]
        sends.append(remote(every, every, ex_send.at[phase], ex_recv.at[phase, 0], sibling))
        return phase, mine, value, coming[::-1]

    def collect(exchanged, refs, nt):
        phase, mine, value, coming = exchanged
        result = few(stacked(value), *get(refs, mine), nt)
        for origin, copy in coming:
            copy.wait_recv()
            arrived = ex[phase, origin]
            value = value + arrived
            result += few(stacked(arrived), *get(refs, origin), nt)
        return result, lane_sum(jnp.where(lane == BLK, value, 0.0))

    def again(exchanged, refs, nt):
        phase, mine, value, coming = exchanged
        result = few(stacked(value), *get(refs, mine), nt)
        for origin, _ in coming:
            result += few(stacked(ex[phase, origin]), *get(refs, origin), nt)
        return result

    tail = WIDE - RIM

    def forward_local(phase, source, sums):
        vs = stacked(source)
        rim = few(vs, xh[tail:, RIM:], xl[tail:, RIM:], True)
        near = exchange(phase, with_sum(rim, sums), 0)
        parts = []
        for i in range(3):
            a, b = i * RIM, (i + 1) * RIM
            parts.append(few(vs[:, :b], xh[a:b, RIM : RIM + b], xl[a:b, RIM : RIM + b], True))
        return near, jnp.concatenate(parts + [rim], axis=1)

    def across_spans(phase, near, first, second, nt):
        value, sums = collect(near, first, nt)
        far = exchange(phase, with_sum(value, sums), 1)
        return far, again(near, second, nt)

    def forward_last(far, local, entering):
        value, sums = collect(far, m2_refs, True)
        moved = few(stacked(entering + value), xh[:, :RIM], xl[:, :RIM], True)
        return local - moved, sums

    def backward(phase, source, beside=None):
        vs = stacked(source)
        rim = few(vs, xh[:, :RIM], xl[:, :RIM], False)
        near = exchange(phase, with_sum(rim, lane_sum(source * source)), 0)
        parts = []
        for i in range(4):
            a, b = i * RIM, (i + 1) * RIM
            parts.append(
                few(vs[:, a:], xh[a:, RIM + a : RIM + b], xl[a:, RIM + a : RIM + b], False)
            )
        local = jnp.concatenate(parts, axis=1)
        far, entering = across_spans(phase + 1, near, p_refs, n_refs, False)
        if beside is not None:
            beside()
        value, sums = collect(far, n2_refs, False)
        moved = few(stacked(entering + value), xh[tail:, RIM:], xl[tail:, RIM:], False)
        return local - moved, sums

    def system_times(step, vector):
        vs = stacked(vector)
        falling = few(vs, lh[:, :RIM], ll[:, :RIM], False)
        copies = []

        def pass_on(way, value, peer):
            nbs[step, way] = value
            copy = remote(
                nbs.at[step, way], nbr.at[step, way],
                nb_send.at[step, way], nb_recv.at[step, way], peer,
            )
            copy.start()
            copies.append(copy)
            sends.append(copy)

        pass_on(0, falling, down)
        last = vector[:, tail:] + few(
            vs[:, tail:], lh[tail:, RIM + tail :], ll[tail:, RIM + tail :], False
        )
        pass_on(1, last, up)
        parts = []
        for i in range(3):
            a, b = i * RIM, (i + 1) * RIM
            parts.append(
                vector[:, a:b]
                + few(vs[:, a:], lh[a:, RIM + a : RIM + b], ll[a:, RIM + a : RIM + b], False)
            )
        upper = jnp.concatenate(parts + [last], axis=1)
        us = stacked(upper)
        parts = []
        for i in range(4):
            a, b = i * RIM, (i + 1) * RIM
            parts.append(few(us[:, :b], lh[a:b, RIM : RIM + b], ll[a:b, RIM : RIM + b], True))
        diagonal = [
            few(vs[:, i * PAD : (i + 1) * PAD], dh[i], dl[i], False) for i in range(ROWS)
        ]
        image = upper + jnp.concatenate(parts, axis=1) + jnp.concatenate(diagonal, axis=1)
        copies[0].wait_recv()
        coming = nbr[step, 0] * flag(row < total - 1)
        corner = coming + few(
            stacked(coming), lh[tail:, RIM + tail :], ll[tail:, RIM + tail :], True
        )
        copies[1].wait_recv()
        before = (nbr[step, 1] + falling) * flag(row > 0)
        image = image + few(stacked(before), lh[:, :RIM], ll[:, :RIM], True)
        return jnp.concatenate([image[:, :tail], image[:, tail:] + corner], axis=1)

    gap = jnp.zeros((columns, PAD - BLK), F32)
    residual = jnp.concatenate(
        [part for i in range(ROWS) for part in (rhs_ref[i], gap)], axis=1
    )
    near, local = forward_local(0, residual, jnp.zeros((columns, 1), F32))

    for t in range(1, cols):
        remote(
            sysl_ref, gathered.at[col], col_send, col_recv, (row, (col + t) % cols)
        ).start()
    others = gathered.at[pl.ds(0, cols - 1)]
    col_every = remote(others, others, col_send, col_recv, up)
    sends.append(col_every)
    own_copy = pltpu.make_async_copy(sysl_ref, gathered.at[col], own_sem)
    own_copy.start()

    def place_system():
        own_copy.wait()
        col_every.wait_recv()
        place(lambda i, k: gathered[k // share, i, k % share])
        for i in range(ROWS):
            high, low = split(dense[i * PAD : (i + 1) * PAD, :])
            lh[i * PAD : (i + 1) * PAD, :] = high
            ll[i * PAD : (i + 1) * PAD, :] = low
            high, low = split(padded(sysd_ref[i]))
            dh[i] = high
            dl[i] = low

    r_iota = lax.broadcasted_iota(jnp.int32, (RIM, RIM), 0)
    c_iota = lax.broadcasted_iota(jnp.int32, (RIM, RIM), 1)
    eye = jnp.where((r_iota == c_iota) & (c_iota % PAD < BLK), 1.0, 0.0).astype(F32)

    def put(refs, s, value):
        high, low = split(value)
        refs[0][s] = high
        refs[1][s] = low

    a_refs, m_refs, r_refs, n_refs, p_refs = (ah, al), (mh, ml), (rh, rl), (nh, nl), (ph, pq)
    m2_refs, n2_refs = (m2h, m2l), (n2h, n2l)

    def flag(condition):
        return jnp.where(condition, 1.0, 0.0).astype(F32)

    def take_in(buf, s):
        put(a_refs, s, jnp.concatenate([unpack(buf[s, 0]), unpack(buf[s, 1])], axis=0))

    take_in(abuf, inner)
    awaited(abuf, at_inner(0, 1), 0, a_send, a_recv)
    take_in(abuf, at_inner(0, 1))
    for x in nearest(chips):
        origin = at_inner(-x, 0)
        awaited(abuf, origin, x, a_send, a_recv)
        hand(abuf, origin, chips + x, a_send, a_recv, sibling)
        take_in(abuf, origin)
    for x in nearest(chips):
        origin = at_inner(-x, 1)
        awaited(abuf, origin, chips + x, a_send, a_recv)
        take_in(abuf, origin)

    level = [get(a_refs, s) for s in range(span)]
    while len(level) > 2:
        level = [split(many(level[n + 1], level[n])) for n in range(0, len(level), 2)]
    across = many(level[1], level[0])
    bbuf[outer, 0] = pack(across[:BLK])
    bbuf[outer, 1] = pack(across[PAD : PAD + BLK])
    for t in reversed(outer_steps):
        hand(bbuf, (outer, core), t, b_send, b_recv, outer_peer(t))

    put(m_refs, span - 1, jnp.zeros((RIM, RIM), F32))
    put(r_refs, span - 1, eye)
    put(n_refs, 0, jnp.zeros((RIM, RIM), F32))
    put(p_refs, 0, eye)

    def chain(t, carry):
        s = span - 1 - t
        right = get(a_refs, s)
        put(m_refs, s - 1, many(get(m_refs, s), right) + flag(s == inner) * eye)
        put(r_refs, s - 1, many(get(r_refs, s), right))
        left = get(a_refs, t)
        put(n_refs, t + 1, many(left, get(n_refs, t)) + flag(t == inner) * eye)
        put(p_refs, t + 1, many(left, get(p_refs, t)))
        return carry

    lax.fori_loop(0, span - 1, chain, 0)

    far, entering = across_spans(1, near, r_refs, m_refs, True)

    for t in outer_steps:
        origin = at_outer(-t)
        awaited(bbuf, (origin, core), t, b_send, b_recv)
        hand(bbuf, (origin, core), spans + t, b_send, b_recv, sibling)
    take_in(bbuf, outer)
    for t in outer_steps:
        origin = at_outer(-t)
        awaited(bbuf, (origin, 1 - core), spans + t, b_send, b_recv)
        take_in(bbuf, origin)
    mine_p = ph[inner].astype(F32) + pq[inner].astype(F32)
    mine_r = rh[inner].astype(F32) + rl[inner].astype(F32)
    put(m2_refs, spans - 1, jnp.zeros((RIM, RIM), F32))
    put(n2_refs, 0, jnp.zeros((RIM, RIM), F32))

    def outer_chain(t, carry):
        s = spans - 1 - t
        put(m2_refs, s - 1, many(get(m2_refs, s), get(a_refs, s)) + flag(s == outer) * mine_p)
        put(n2_refs, t + 1, many(get(a_refs, t), get(n2_refs, t)) + flag(t == outer) * mine_r)
        return carry

    lax.fori_loop(0, spans - 1, outer_chain, 0)

    solved, _ = forward_last(far, local, entering)
    direction, energy = backward(2, solved, place_system)
    answer = jnp.zeros_like(residual)
    for step in range(ITERS):
        phase = 4 * (step + 1)
        image = system_times(step, direction)
        near, local = forward_local(phase, image, lane_sum(direction * image))
        far, entering = across_spans(phase + 1, near, r_refs, m_refs, True)
        change, curvature = forward_last(far, local, entering)
        alpha = energy / curvature
        answer = answer + alpha * direction
        residual = residual - alpha * image
        solved = solved - alpha * change
        precond, energy_next = backward(phase + 2, solved)
        direction = precond + (energy_next / energy) * direction
        energy = energy_next

    for i in range(ROWS):
        lanes = slice(i * PAD, (i + 1) * PAD)
        out_ref[0, i] = answer[:, lanes]
        out_ref[1, i] = residual[:, lanes]
        out_ref[2, i] = direction[:, lanes]
    for copy in sends:
        copy.wait_send()


def per_device(
    spans, cols, rhs, system_lower, system_diag, factor_lower, diag_inverse, neighbours, counts
):
    rows, width, columns = rhs.shape
    vmem = pl.BlockSpec(memory_space=pltpu.VMEM)
    phases = 4 * (ITERS + 1)
    half = lambda: pltpu.VMEM((GROUP, RIM, RIM), BF16)
    most = max(GROUP, spans)
    tall = lambda: pltpu.VMEM((most, RIM, RIM), BF16)
    dma = pltpu.SemaphoreType.DMA
    outs = pl.pallas_call(
        functools.partial(kernel, GROUP, spans, cols),
        out_shape=jax.ShapeDtypeStruct((3, rows, columns, PAD), F32),
        in_specs=[pl.BlockSpec(memory_space=pltpu.SMEM)] * 2
        + [vmem, pl.BlockSpec(memory_space=pl.ANY)]
        + [vmem] * 3,
        out_specs=vmem,
        scratch_shapes=[
            pltpu.VMEM((WIDE, RIM + WIDE), F32),
            pltpu.VMEM((WIDE, RIM + WIDE), BF16),
            pltpu.VMEM((WIDE, RIM + WIDE), BF16),
            pltpu.VMEM((WIDE, RIM + WIDE), BF16),
            pltpu.VMEM((WIDE, RIM + WIDE), BF16),
            pltpu.VMEM((ROWS, PAD, PAD), BF16),
            pltpu.VMEM((ROWS, PAD, PAD), BF16),
            pltpu.VMEM((cols,) + system_lower.shape, F32),
            pltpu.VMEM((GROUP, 2, PACKED, PAD), F32),
            pltpu.VMEM((spans, 2, PACKED, PAD), F32),
            tall(), tall(),
            half(), half(), half(), half(), half(), half(), half(), half(),
            tall(), tall(), tall(), tall(),
            pltpu.VMEM((phases, most, columns, RIM), F32),
            pltpu.VMEM((ITERS, 2, columns, RIM), F32),
            pltpu.VMEM((ITERS, 2, columns, RIM), F32),
            dma, dma, dma, dma((GROUP,)), dma((GROUP,)), dma((2 * spans,)), dma((2 * spans,)),
            dma((phases,)), dma((phases, most - 1)), dma((ITERS, 2)), dma((ITERS, 2)),
        ],
        compiler_params=pltpu.CompilerParams(
            collective_id=0, has_side_effects=True, vmem_limit_bytes=60 * 1024 * 1024
        ),
    )(
        neighbours, counts, jnp.transpose(rhs, (0, 2, 1)), system_lower, system_diag,
        factor_lower, diag_inverse,
    )
    return tuple(jnp.transpose(outs[n, :, :, :width], (0, 2, 1)) for n in range(3))


def solution(mesh):
    in_specs = (
        P("row", None, "col"),
        P("row", "col", None, None),
        P("row", None, None),
        P("row", None, None, None),
        P("row", None, None),
        P("row", None),
        P("row"),
    )
    out_specs = (P("row", None, "col"), P("row", None, "col"), P("row", None, "col"))
    return jax.shard_map(
        functools.partial(per_device, mesh.shape["row"] // GROUP, mesh.shape["col"]),
        mesh=mesh, in_specs=in_specs, out_specs=out_specs, check_vma=False,
    )
```

```python
import functools

import jax
import jax.numpy as jnp
from jax import lax
from jax.experimental import pallas as pl
from jax.experimental.pallas import tpu as pltpu
from jax.sharding import PartitionSpec as P

ITERS = 2
GROUP = 8
BLK = 72
ROWS = 8
PAD = 128
WIDE = ROWS * PAD
RIM = 2 * PAD
PACKED = BLK + 16
F32 = jnp.float32
BF16 = jnp.bfloat16
MESH = pl.DeviceIdType.MESH


def split(x):
    high = x.astype(BF16)
    return high, (x - high.astype(F32)).astype(BF16)


def dot(a, b, nt):
    return lax.dot_general(
        a, b, (((1,), (1 if nt else 0,)), ((), ())), preferred_element_type=F32
    )


def stacked(v):
    high, low = split(v)
    return jnp.concatenate([high, low], axis=0)


def few(vs, high, low, nt):
    rows = vs.shape[0] // 2
    both = dot(vs, high, nt)
    return both[:rows] + both[rows:] + dot(vs[:rows], low, nt)


def many(a, b, nt=False):
    return dot(a[0], b[0], nt) + (dot(a[0], b[1], nt) + dot(a[1], b[0], nt))


def nearest(count):
    return sorted(range(1, count), key=lambda t: min(t, count - t))


def pack(half):
    lane = lax.broadcasted_iota(jnp.int32, (BLK, PAD), 1)
    turned = pltpu.roll(half[:, PAD:], BLK, 1)
    top = jnp.where(lane < BLK, half[:, :PAD], turned)
    rest = jnp.where(lane < 16, turned, 0.0)
    first = rest[:8]
    for g in range(1, 8):
        first += pltpu.roll(rest[8 * g : 8 * g + 8], 16 * g, 1)
    return jnp.concatenate([top, first, rest[64:]], axis=0)


def unpack(packed):
    lane = lax.broadcasted_iota(jnp.int32, (BLK, PAD), 1)
    top, first, last = packed[:BLK], packed[BLK : BLK + 8], packed[BLK + 8 :]
    edge = PAD - BLK
    rest = [pltpu.roll(first, (edge - 16 * g) % PAD, 1) for g in range(8)]
    rest = jnp.concatenate(rest + [pltpu.roll(last, edge, 1)], axis=0)
    right = jnp.where(lane < edge, pltpu.roll(top, edge, 1), jnp.where(lane < BLK, rest, 0.0))
    left = jnp.where(lane < BLK, top, 0.0)
    value = jnp.concatenate([left, right], axis=1)
    return jnp.concatenate([value, jnp.zeros((PAD - BLK, RIM), F32)], axis=0)


def kernel(
    span, spans, cols, neighbours_ref, counts_ref, rhs_ref, sysl_ref, sysd_ref, fac_ref, dinv_ref,
    out_ref,
    dense, xh, xl, lh, ll, dh, dl, gathered, abuf, bbuf, qbuf, ah, al, th, tl, wh, wl,
    mh, ml, rh, rl, nh, nl, ph, pq, m2h, m2l, n2h, n2l, ex, nbs, nbr,
    own_sem, col_send, col_recv, a_send, a_recv, b_send, b_recv, q_send, q_recv, ex_send, ex_recv, nb_send, nb_recv,
):
    row, col = lax.axis_index("row"), lax.axis_index("col")
    total = span * spans
    outer, inner = row // span, row % span
    share = sysl_ref.shape[1]
    columns = rhs_ref.shape[1]
    chips = span // 2
    chip, core = inner // 2, inner % 2

    def at_inner(x, c):
        return ((chip + x + chips) % chips) * 2 + (core + c + 2) % 2

    def at_outer(t):
        return (outer + t + spans) % spans

    def inner_peer(x, c):
        return (outer * span + at_inner(x, c), col)

    def outer_peer(t):
        return (at_outer(t) * span + inner, col)

    inner_steps = [(x, c) for x in [0] + nearest(chips) for c in range(2)][1:]
    outer_steps = nearest(spans)
    up, down = ((row + 1) % total, col), ((row + total - 1) % total, col)
    sibling = inner_peer(0, 1)

    barrier = pltpu.get_barrier_semaphore()
    greeted = (
        [inner_peer(*t) for t in inner_steps]
        + [outer_peer(t) for t in outer_steps]
        + [(row, (col + t) % cols) for t in range(1, cols)]
        + [up, down]
    )
    for peer in greeted:
        pl.semaphore_signal(barrier, inc=1, device_id=peer, device_id_type=MESH)

    sends = []

    def remote(source, target, send_sem, recv_sem, peer):
        return pltpu.make_async_remote_copy(
            src_ref=source, dst_ref=target, send_sem=send_sem, recv_sem=recv_sem,
            device_id=peer, device_id_type=MESH,
        )

    def place(block_of):
        def one(i, carry):
            blocks = [block_of(i, k) for k in range(8)]
            at = pl.multiple_of(i * PAD, PAD)
            places = [
                jnp.where(k < counts_ref[i], neighbours_ref[i, k] - row * ROWS + 2, -1)
                for k in range(8)
            ]
            for s in range(ROWS + 2):
                value = jnp.where(places[0] == s, 1.0, 0.0) * blocks[0]
                for k in range(1, 8):
                    value += jnp.where(places[k] == s, 1.0, 0.0) * blocks[k]
                dense[pl.ds(at, BLK), s * PAD : s * PAD + BLK] = value
            return carry

        lax.fori_loop(0, ROWS, one, 0)

    def padded(block):
        wide = jnp.concatenate([block, jnp.zeros((BLK, PAD - BLK), F32)], axis=1)
        return jnp.concatenate([wide, jnp.zeros((PAD - BLK, PAD), F32)], axis=0)

    dense[...] = jnp.zeros_like(dense)
    place(lambda i, k: fac_ref[i, k])

    inverses = [padded(dinv_ref[i]) for i in range(ROWS)]
    scaled = [
        many(split(inverses[i]), split(dense[i * PAD : (i + 1) * PAD, : RIM + i * PAD]))
        for i in range(ROWS)
    ]
    nothing = jnp.zeros((PAD, PAD), F32)
    for i in range(0, ROWS, 2):
        width = RIM + i * PAD
        first, second = scaled[i], scaled[i + 1][:, :width]
        taken = many(
            split(scaled[i + 1][:, width:]),
            split(jnp.concatenate([first, inverses[i]], axis=1)),
        )
        rows = jnp.concatenate([first, second - taken[:, :width]], axis=0)
        corner = jnp.concatenate(
            [
                jnp.concatenate([inverses[i], nothing], axis=1),
                jnp.concatenate([-taken[:, width:], inverses[i + 1]], axis=1),
            ],
            axis=0,
        )
        edge = rows[:, :RIM]
        if i > 0:
            step = many(split(rows[:, RIM:]), (xh[: i * PAD, :width], xl[: i * PAD, :width]))
            edge = edge - step[:, :RIM]
            body = [edge, -step[:, RIM:], corner]
        else:
            body = [edge, corner]
        if i < ROWS - 2:
            body.append(jnp.zeros((2 * PAD, WIDE - (i + 2) * PAD), F32))
        high, low = split(jnp.concatenate(body, axis=1))
        xh[i * PAD : (i + 2) * PAD, :] = high
        xl[i * PAD : (i + 2) * PAD, :] = low
    abuf[inner, 0] = pack(-edge[:BLK, :])
    abuf[inner, 1] = pack(-edge[PAD : PAD + BLK, :])

    pl.semaphore_wait(barrier, len(greeted))

    def hand(buf, slot, n, send, recv, peer):
        copy = remote(buf.at[slot], buf.at[slot], send.at[n], recv.at[n], peer)
        copy.start()
        sends.append(copy)

    def awaited(buf, slot, n, send, recv):
        remote(buf.at[slot], buf.at[slot], send.at[n], recv.at[n], sibling).wait_recv()

    def give(buf, send, recv):
        for x in reversed(nearest(chips)):
            hand(buf, inner, x, send, recv, inner_peer(x, 0))
        hand(buf, inner, 0, send, recv, sibling)

    def take(buf, send, recv, use):
        use(inner)
        awaited(buf, at_inner(0, 1), 0, send, recv)
        use(at_inner(0, 1))
        for x in nearest(chips):
            origin = at_inner(-x, 0)
            awaited(buf, origin, x, send, recv)
            hand(buf, origin, chips + x, send, recv, sibling)
            use(origin)
        for x in nearest(chips):
            origin = at_inner(-x, 1)
            awaited(buf, origin, chips + x, send, recv)
            use(origin)

    give(abuf, a_send, a_recv)

    lane = lax.broadcasted_iota(jnp.int32, (columns, RIM), 1)

    def with_sum(value, sums):
        return jnp.where(lane == BLK, sums, jnp.where(lane % PAD < BLK, value, 0.0))

    def lane_sum(value):
        return jnp.sum(value, axis=1, keepdims=True)

    def get(refs, s):
        return refs[0][s], refs[1][s]

    def exchange(phase, value, level):
        buf = ex.at[phase]
        mine, steps, peer_of, count = (
            (inner, inner_steps, lambda t: inner_peer(*t), span)
            if level == 0
            else (outer, outer_steps, outer_peer, spans)
        )
        buf[mine] = value
        coming = []
        for n, t in reversed(list(enumerate(steps))):
            sems = ex_send.at[phase], ex_recv.at[phase, n]
            remote(buf.at[mine], buf.at[mine], *sems, peer_of(t)).start()
            origin = at_inner(-t[0], -t[1]) if level == 0 else at_outer(-t)
            coming.append((origin, remote(buf.at[origin], buf.at[origin], *sems, sibling)))
        every = buf.at[pl.ds(0, count - 1)]
        sends.append(remote(every, every, ex_send.at[phase], ex_recv.at[phase, 0], sibling))
        return phase, mine, value, coming[::-1]

    def collect(exchanged, refs, nt):
        phase, mine, value, coming = exchanged
        result = few(stacked(value), *get(refs, mine), nt)
        for origin, copy in coming:
            copy.wait_recv()
            arrived = ex[phase, origin]
            value = value + arrived
            result += few(stacked(arrived), *get(refs, origin), nt)
        return result, lane_sum(jnp.where(lane == BLK, value, 0.0))

    def again(exchanged, refs, nt):
        phase, mine, value, coming = exchanged
        result = few(stacked(value), *get(refs, mine), nt)
        for origin, _ in coming:
            result += few(stacked(ex[phase, origin]), *get(refs, origin), nt)
        return result

    tail = WIDE - RIM

    def forward_local(phase, source, sums):
        vs = stacked(source)
        rim = few(vs, xh[tail:, RIM:], xl[tail:, RIM:], True)
        near = exchange(phase, with_sum(rim, sums), 0)
        parts = []
        for i in range(3):
            a, b = i * RIM, (i + 1) * RIM
            parts.append(few(vs[:, :b], xh[a:b, RIM : RIM + b], xl[a:b, RIM : RIM + b], True))
        return near, jnp.concatenate(parts + [rim], axis=1)

    def forward_across(phase, near, local):
        value, sums = collect(near, r_refs, True)
        far = exchange(phase + 1, with_sum(value, sums), 1)
        entering = again(near, m_refs, True)
        local = local - few(stacked(entering), xh[:, :RIM], xl[:, :RIM], True)
        rim = few(stacked(local), xh[:, :RIM], xl[:, :RIM], False)
        return far, local, exchange(phase + 2, with_sum(rim, 0.0), 0)

    def backward_inside(back):
        value, _ = collect(back, p_refs, False)
        return value, again(back, n_refs, False)

    def forward_last(far, local, falling):
        value, sums = collect(far, m2_refs, True)
        vs = stacked(value)
        local = local - few(vs, wh[...], wl[...], True)
        spanned = falling[0] - few(vs, *get(t_refs, 0), False)
        own = falling[1] - few(vs, *get(t_refs, 1), False)
        return (local, spanned, own), sums

    def backward(phase, state, beside=None):
        source, spanned, own = state
        far = exchange(phase + 3, with_sum(spanned, lane_sum(source * source)), 1)
        vs = stacked(source)
        parts = []
        for i in range(4):
            a, b = i * RIM, (i + 1) * RIM
            parts.append(
                few(vs[:, a:], xh[a:, RIM + a : RIM + b], xl[a:, RIM + a : RIM + b], False)
            )
        local = jnp.concatenate(parts, axis=1)
        if beside is not None:
            beside()
        value, sums = collect(far, n2_refs, False)
        energy = exchange(phase + 4, jnp.where(lane == BLK, sums, 0.0), 0)
        moved = few(stacked(own + value), xh[tail:, RIM:], xl[tail:, RIM:], False)
        return local - moved, energy

    def total_of(exchanged):
        phase, _, value, coming = exchanged
        for origin, copy in coming:
            copy.wait_recv()
            value = value + ex[phase, origin]
        return lane_sum(jnp.where(lane == BLK, value, 0.0))

    def system_times(step, vector):
        vs = stacked(vector)
        falling = few(vs, lh[:, :RIM], ll[:, :RIM], False)
        copies = []

        def pass_on(way, value, peer):
            nbs[step, way] = value
            copy = remote(
                nbs.at[step, way], nbr.at[step, way],
                nb_send.at[step, way], nb_recv.at[step, way], peer,
            )
            copy.start()
            copies.append(copy)
            sends.append(copy)

        pass_on(0, falling, down)
        last = vector[:, tail:] + few(
            vs[:, tail:], lh[tail:, RIM + tail :], ll[tail:, RIM + tail :], False
        )
        pass_on(1, last, up)
        parts = []
        for i in range(3):
            a, b = i * RIM, (i + 1) * RIM
            parts.append(
                vector[:, a:b]
                + few(vs[:, a:], lh[a:, RIM + a : RIM + b], ll[a:, RIM + a : RIM + b], False)
            )
        upper = jnp.concatenate(parts + [last], axis=1)
        us = stacked(upper)
        parts = []
        for i in range(4):
            a, b = i * RIM, (i + 1) * RIM
            parts.append(few(us[:, :b], lh[a:b, RIM : RIM + b], ll[a:b, RIM : RIM + b], True))
        diagonal = [
            few(vs[:, i * PAD : (i + 1) * PAD], dh[i], dl[i], False) for i in range(ROWS)
        ]
        image = upper + jnp.concatenate(parts, axis=1) + jnp.concatenate(diagonal, axis=1)
        copies[0].wait_recv()
        coming = nbr[step, 0] * flag(row < total - 1)
        corner = coming + few(
            stacked(coming), lh[tail:, RIM + tail :], ll[tail:, RIM + tail :], True
        )
        copies[1].wait_recv()
        before = (nbr[step, 1] + falling) * flag(row > 0)
        image = image + few(stacked(before), lh[:, :RIM], ll[:, :RIM], True)
        return jnp.concatenate([image[:, :tail], image[:, tail:] + corner], axis=1)

    gap = jnp.zeros((columns, PAD - BLK), F32)
    residual = jnp.concatenate(
        [part for i in range(ROWS) for part in (rhs_ref[i], gap)], axis=1
    )
    near, local = forward_local(0, residual, jnp.zeros((columns, 1), F32))

    for t in range(1, cols):
        remote(
            sysl_ref, gathered.at[col], col_send, col_recv, (row, (col + t) % cols)
        ).start()
    others = gathered.at[pl.ds(0, cols - 1)]
    col_every = remote(others, others, col_send, col_recv, up)
    sends.append(col_every)
    own_copy = pltpu.make_async_copy(sysl_ref, gathered.at[col], own_sem)
    own_copy.start()

    def place_system():
        own_copy.wait()
        col_every.wait_recv()
        place(lambda i, k: gathered[k // share, i, k % share])
        for i in range(ROWS):
            high, low = split(dense[i * PAD : (i + 1) * PAD, :])
            lh[i * PAD : (i + 1) * PAD, :] = high
            ll[i * PAD : (i + 1) * PAD, :] = low
            high, low = split(padded(sysd_ref[i]))
            dh[i] = high
            dl[i] = low

    r_iota = lax.broadcasted_iota(jnp.int32, (RIM, RIM), 0)
    c_iota = lax.broadcasted_iota(jnp.int32, (RIM, RIM), 1)
    eye = jnp.where((r_iota == c_iota) & (c_iota % PAD < BLK), 1.0, 0.0).astype(F32)

    def put(refs, s, value):
        high, low = split(value)
        refs[0][s] = high
        refs[1][s] = low

    a_refs, m_refs, r_refs, n_refs, p_refs = (ah, al), (mh, ml), (rh, rl), (nh, nl), (ph, pq)
    m2_refs, n2_refs, t_refs = (m2h, m2l), (n2h, n2l), (th, tl)

    def flag(condition):
        return jnp.where(condition, 1.0, 0.0).astype(F32)

    def take_in(buf, s):
        put(a_refs, s, jnp.concatenate([unpack(buf[s, 0]), unpack(buf[s, 1])], axis=0))

    edge = xh[:, :RIM].astype(F32) + xl[:, :RIM].astype(F32)
    square = many(split(edge.T), (xh[:, :RIM], xl[:, :RIM]))
    qbuf[inner, 0] = pack(square[:BLK])
    qbuf[inner, 1] = pack(square[PAD : PAD + BLK])

    take(abuf, a_send, a_recv, functools.partial(take_in, abuf))

    level = [get(a_refs, s) for s in range(span)]
    while len(level) > 2:
        level = [split(many(level[n + 1], level[n])) for n in range(0, len(level), 2)]
    across = many(level[1], level[0])
    bbuf[outer, 0] = pack(across[:BLK])
    bbuf[outer, 1] = pack(across[PAD : PAD + BLK])
    for t in reversed(outer_steps):
        hand(bbuf, (outer, core), t, b_send, b_recv, outer_peer(t))

    give(qbuf, q_send, q_recv)

    put(m_refs, span - 1, jnp.zeros((RIM, RIM), F32))
    put(r_refs, span - 1, eye)
    put(n_refs, 0, jnp.zeros((RIM, RIM), F32))
    put(p_refs, 0, eye)

    def chain(t, carry):
        s = span - 1 - t
        right = get(a_refs, s)
        put(m_refs, s - 1, many(get(m_refs, s), right) + flag(s == inner) * eye)
        put(r_refs, s - 1, many(get(r_refs, s), right))
        left = get(a_refs, t)
        put(n_refs, t + 1, many(left, get(n_refs, t)) + flag(t == inner) * eye)
        put(p_refs, t + 1, many(left, get(p_refs, t)))
        return carry

    lax.fori_loop(0, span - 1, chain, 0)

    far, local, back = forward_across(0, near, local)

    entered = [jnp.zeros((RIM, RIM), F32), jnp.zeros((RIM, RIM), F32)]

    def quadratic(s):
        whole = jnp.concatenate([unpack(qbuf[s, 0]), unpack(qbuf[s, 1])], axis=0)
        half = split(many(split(whole), get(p_refs, s)).T)
        entered[0] += many(half, get(p_refs, s))
        entered[1] += many(half, get(n_refs, s))

    take(qbuf, q_send, q_recv, quadratic)
    put(t_refs, 0, entered[0])
    put(t_refs, 1, entered[1])
    high, low = split(many((xh[:, :RIM], xl[:, :RIM]), get(p_refs, inner)))
    wh[...] = high
    wl[...] = low
    falling = backward_inside(back)

    for t in outer_steps:
        origin = at_outer(-t)
        awaited(bbuf, (origin, core), t, b_send, b_recv)
        hand(bbuf, (origin, core), spans + t, b_send, b_recv, sibling)
    take_in(bbuf, outer)
    for t in outer_steps:
        origin = at_outer(-t)
        awaited(bbuf, (origin, 1 - core), spans + t, b_send, b_recv)
        take_in(bbuf, origin)
    mine_r = rh[inner].astype(F32) + rl[inner].astype(F32)
    put(m2_refs, spans - 1, jnp.zeros((RIM, RIM), F32))
    put(n2_refs, 0, jnp.zeros((RIM, RIM), F32))

    def outer_chain(t, carry):
        s = spans - 1 - t
        put(m2_refs, s - 1, many(get(m2_refs, s), get(a_refs, s)) + flag(s == outer) * eye)
        put(n2_refs, t + 1, many(get(a_refs, t), get(n2_refs, t)) + flag(t == outer) * mine_r)
        return carry

    lax.fori_loop(0, spans - 1, outer_chain, 0)

    state, _ = forward_last(far, local, falling)
    direction, waiting = backward(0, state, place_system)
    image = system_times(0, direction)
    energy = total_of(waiting)
    answer = jnp.zeros_like(residual)
    for step in range(ITERS):
        phase = 5 * (step + 1)
        near, local = forward_local(phase, image, lane_sum(direction * image))
        far, local, back = forward_across(phase, near, local)
        falling = backward_inside(back)
        change, curvature = forward_last(far, local, falling)
        alpha = energy / curvature
        state = tuple(old - alpha * new for old, new in zip(state, change))
        precond, waiting = backward(phase, state)
        answer = answer + alpha * direction
        residual = residual - alpha * image
        if step < ITERS - 1:
            following = system_times(step + 1, precond)
        energy_next = total_of(waiting)
        ratio = energy_next / energy
        direction = precond + ratio * direction
        if step < ITERS - 1:
            image = following + ratio * image
        energy = energy_next

    for i in range(ROWS):
        lanes = slice(i * PAD, (i + 1) * PAD)
        out_ref[0, i] = answer[:, lanes]
        out_ref[1, i] = residual[:, lanes]
        out_ref[2, i] = direction[:, lanes]
    for copy in sends:
        copy.wait_send()


def per_device(
    spans, cols, rhs, system_lower, system_diag, factor_lower, diag_inverse, neighbours, counts
):
    rows, width, columns = rhs.shape
    vmem = pl.BlockSpec(memory_space=pltpu.VMEM)
    phases = 5 * (ITERS + 1)
    half = lambda: pltpu.VMEM((GROUP, RIM, RIM), BF16)
    most = max(GROUP, spans)
    tall = lambda: pltpu.VMEM((most, RIM, RIM), BF16)
    dma = pltpu.SemaphoreType.DMA
    outs = pl.pallas_call(
        functools.partial(kernel, GROUP, spans, cols),
        out_shape=jax.ShapeDtypeStruct((3, rows, columns, PAD), F32),
        in_specs=[pl.BlockSpec(memory_space=pltpu.SMEM)] * 2
        + [vmem, pl.BlockSpec(memory_space=pl.ANY)]
        + [vmem] * 3,
        out_specs=vmem,
        scratch_shapes=[
            pltpu.VMEM((WIDE, RIM + WIDE), F32),
            pltpu.VMEM((WIDE, RIM + WIDE), BF16),
            pltpu.VMEM((WIDE, RIM + WIDE), BF16),
            pltpu.VMEM((WIDE, RIM + WIDE), BF16),
            pltpu.VMEM((WIDE, RIM + WIDE), BF16),
            pltpu.VMEM((ROWS, PAD, PAD), BF16),
            pltpu.VMEM((ROWS, PAD, PAD), BF16),
            pltpu.VMEM((cols,) + system_lower.shape, F32),
            pltpu.VMEM((GROUP, 2, PACKED, PAD), F32),
            pltpu.VMEM((spans, 2, PACKED, PAD), F32),
            pltpu.VMEM((GROUP, 2, PACKED, PAD), F32),
            tall(), tall(),
            pltpu.VMEM((2, RIM, RIM), BF16), pltpu.VMEM((2, RIM, RIM), BF16),
            pltpu.VMEM((WIDE, RIM), BF16), pltpu.VMEM((WIDE, RIM), BF16),
            half(), half(), half(), half(), half(), half(), half(), half(),
            tall(), tall(), tall(), tall(),
            pltpu.VMEM((phases, most, columns, RIM), F32),
            pltpu.VMEM((ITERS, 2, columns, RIM), F32),
            pltpu.VMEM((ITERS, 2, columns, RIM), F32),
            dma, dma, dma, dma((GROUP,)), dma((GROUP,)), dma((2 * spans,)), dma((2 * spans,)),
            dma((GROUP,)), dma((GROUP,)),
            dma((phases,)), dma((phases, most - 1)), dma((ITERS, 2)), dma((ITERS, 2)),
        ],
        compiler_params=pltpu.CompilerParams(
            collective_id=0, has_side_effects=True, vmem_limit_bytes=60 * 1024 * 1024
        ),
    )(
        neighbours, counts, jnp.transpose(rhs, (0, 2, 1)), system_lower, system_diag,
        factor_lower, diag_inverse,
    )
    return tuple(jnp.transpose(outs[n, :, :, :width], (0, 2, 1)) for n in range(3))


def solution(mesh):
    in_specs = (
        P("row", None, "col"),
        P("row", "col", None, None),
        P("row", None, None),
        P("row", None, None, None),
        P("row", None, None),
        P("row", None),
        P("row"),
    )
    out_specs = (P("row", None, "col"), P("row", None, "col"), P("row", None, "col"))
    return jax.shard_map(
        functools.partial(per_device, mesh.shape["row"] // GROUP, mesh.shape["col"]),
        mesh=mesh, in_specs=in_specs, out_specs=out_specs, check_vma=False,
    )
```

```python
import functools

import jax
import jax.numpy as jnp
from jax import lax
from jax.experimental import pallas as pl
from jax.experimental.pallas import tpu as pltpu
from jax.sharding import PartitionSpec as P

ITERS = 2
GROUP = 8
BLK = 72
ROWS = 8
PAD = 128
WIDE = ROWS * PAD
RIM = 2 * PAD
PACKED = BLK + 16
F32 = jnp.float32
BF16 = jnp.bfloat16
MESH = pl.DeviceIdType.MESH


def split(x):
    high = x.astype(BF16)
    return high, (x - high.astype(F32)).astype(BF16)


def dot(a, b, nt):
    return lax.dot_general(
        a, b, (((1,), (1 if nt else 0,)), ((), ())), preferred_element_type=F32
    )


def stacked(v):
    high, low = split(v)
    return jnp.concatenate([high, low], axis=0)


def few(vs, high, low, nt):
    rows = vs.shape[0] // 2
    both = dot(vs, high, nt)
    return both[:rows] + both[rows:] + dot(vs[:rows], low, nt)


def many(a, b, nt=False):
    return dot(a[0], b[0], nt) + (dot(a[0], b[1], nt) + dot(a[1], b[0], nt))


def nearest(count):
    return sorted(range(1, count), key=lambda t: min(t, count - t))


def pack(half):
    lane = lax.broadcasted_iota(jnp.int32, (BLK, PAD), 1)
    turned = pltpu.roll(half[:, PAD:], BLK, 1)
    top = jnp.where(lane < BLK, half[:, :PAD], turned)
    rest = jnp.where(lane < 16, turned, 0.0)
    first = rest[:8]
    for g in range(1, 8):
        first += pltpu.roll(rest[8 * g : 8 * g + 8], 16 * g, 1)
    return jnp.concatenate([top, first, rest[64:]], axis=0)


def unpack(packed):
    lane = lax.broadcasted_iota(jnp.int32, (BLK, PAD), 1)
    top, first, last = packed[:BLK], packed[BLK : BLK + 8], packed[BLK + 8 :]
    edge = PAD - BLK
    rest = [pltpu.roll(first, (edge - 16 * g) % PAD, 1) for g in range(8)]
    rest = jnp.concatenate(rest + [pltpu.roll(last, edge, 1)], axis=0)
    right = jnp.where(lane < edge, pltpu.roll(top, edge, 1), jnp.where(lane < BLK, rest, 0.0))
    left = jnp.where(lane < BLK, top, 0.0)
    value = jnp.concatenate([left, right], axis=1)
    return jnp.concatenate([value, jnp.zeros((PAD - BLK, RIM), F32)], axis=0)


def kernel(
    span, spans, cols, neighbours_ref, counts_ref, rhs_ref, sysl_ref, sysd_ref, fac_ref, dinv_ref,
    out_ref,
    dense, xh, xl, lh, ll, dh, dl, gathered, abuf, bbuf, qbuf, ah, al, th, tl, wh, wl,
    mh, ml, rh, rl, nh, nl, ph, pq, m2h, m2l, n2h, n2l, ex, nbs, nbr,
    own_sem, col_send, col_recv, a_send, a_recv, b_send, b_recv, q_send, q_recv, ex_send, ex_recv, nb_send, nb_recv,
):
    row, col = lax.axis_index("row"), lax.axis_index("col")
    total = span * spans
    outer, inner = row // span, row % span
    share = sysl_ref.shape[1]
    columns = rhs_ref.shape[1]
    chips = span // 2
    chip, core = inner // 2, inner % 2

    def at_inner(x, c):
        return ((chip + x + chips) % chips) * 2 + (core + c + 2) % 2

    def at_outer(t):
        return (outer + t + spans) % spans

    def inner_peer(x, c):
        return (outer * span + at_inner(x, c), col)

    def outer_peer(t):
        return (at_outer(t) * span + inner, col)

    inner_steps = [(x, c) for x in [0] + nearest(chips) for c in range(2)][1:]
    outer_steps = nearest(spans)
    up, down = ((row + 1) % total, col), ((row + total - 1) % total, col)
    sibling = inner_peer(0, 1)

    barrier = pltpu.get_barrier_semaphore()
    greeted = (
        [inner_peer(*t) for t in inner_steps]
        + [outer_peer(t) for t in outer_steps]
        + [(row, (col + t) % cols) for t in range(1, cols)]
        + [up, down]
    )
    for peer in greeted:
        pl.semaphore_signal(barrier, inc=1, device_id=peer, device_id_type=MESH)

    sends = []

    def remote(source, target, send_sem, recv_sem, peer):
        return pltpu.make_async_remote_copy(
            src_ref=source, dst_ref=target, send_sem=send_sem, recv_sem=recv_sem,
            device_id=peer, device_id_type=MESH,
        )

    def place(block_of):
        def one(i, carry):
            blocks = [block_of(i, k) for k in range(8)]
            at = pl.multiple_of(i * PAD, PAD)
            places = [
                jnp.where(k < counts_ref[i], neighbours_ref[i, k] - row * ROWS + 2, -1)
                for k in range(8)
            ]
            for s in range(ROWS + 2):
                value = jnp.where(places[0] == s, 1.0, 0.0) * blocks[0]
                for k in range(1, 8):
                    value += jnp.where(places[k] == s, 1.0, 0.0) * blocks[k]
                dense[pl.ds(at, BLK), s * PAD : s * PAD + BLK] = value
            return carry

        lax.fori_loop(0, ROWS, one, 0)

    def padded(block):
        wide = jnp.concatenate([block, jnp.zeros((BLK, PAD - BLK), F32)], axis=1)
        return jnp.concatenate([wide, jnp.zeros((PAD - BLK, PAD), F32)], axis=0)

    dense[...] = jnp.zeros_like(dense)
    place(lambda i, k: fac_ref[i, k])

    inverses = [padded(dinv_ref[i]) for i in range(ROWS)]
    scaled = [
        many(split(inverses[i]), split(dense[i * PAD : (i + 1) * PAD, : RIM + i * PAD]))
        for i in range(ROWS)
    ]
    nothing = jnp.zeros((PAD, PAD), F32)
    for i in range(0, ROWS, 2):
        width = RIM + i * PAD
        first, second = scaled[i], scaled[i + 1][:, :width]
        taken = many(
            split(scaled[i + 1][:, width:]),
            split(jnp.concatenate([first, inverses[i]], axis=1)),
        )
        rows = jnp.concatenate([first, second - taken[:, :width]], axis=0)
        corner = jnp.concatenate(
            [
                jnp.concatenate([inverses[i], nothing], axis=1),
                jnp.concatenate([-taken[:, width:], inverses[i + 1]], axis=1),
            ],
            axis=0,
        )
        edge = rows[:, :RIM]
        if i > 0:
            step = many(split(rows[:, RIM:]), (xh[: i * PAD, :width], xl[: i * PAD, :width]))
            edge = edge - step[:, :RIM]
            body = [edge, -step[:, RIM:], corner]
        else:
            body = [edge, corner]
        if i < ROWS - 2:
            body.append(jnp.zeros((2 * PAD, WIDE - (i + 2) * PAD), F32))
        high, low = split(jnp.concatenate(body, axis=1))
        xh[i * PAD : (i + 2) * PAD, :] = high
        xl[i * PAD : (i + 2) * PAD, :] = low
    abuf[inner, 0] = pack(-edge[:BLK, :])
    abuf[inner, 1] = pack(-edge[PAD : PAD + BLK, :])

    pl.semaphore_wait(barrier, len(greeted))

    def hand(buf, slot, n, send, recv, peer):
        copy = remote(buf.at[slot], buf.at[slot], send.at[n], recv.at[n], peer)
        copy.start()
        sends.append(copy)

    def awaited(buf, slot, n, send, recv):
        remote(buf.at[slot], buf.at[slot], send.at[n], recv.at[n], sibling).wait_recv()

    def give(buf, send, recv):
        for x in reversed(nearest(chips)):
            hand(buf, inner, x, send, recv, inner_peer(x, 0))
        hand(buf, inner, 0, send, recv, sibling)

    def take(buf, send, recv, use):
        use(inner)
        awaited(buf, at_inner(0, 1), 0, send, recv)
        use(at_inner(0, 1))
        for x in nearest(chips):
            origin = at_inner(-x, 0)
            awaited(buf, origin, x, send, recv)
            hand(buf, origin, chips + x, send, recv, sibling)
            use(origin)
        for x in nearest(chips):
            origin = at_inner(-x, 1)
            awaited(buf, origin, chips + x, send, recv)
            use(origin)

    give(abuf, a_send, a_recv)

    lane = lax.broadcasted_iota(jnp.int32, (columns, RIM), 1)

    def with_sum(value, sums):
        return jnp.where(lane == BLK, sums, jnp.where(lane % PAD < BLK, value, 0.0))

    def lane_sum(value):
        return jnp.sum(value, axis=1, keepdims=True)

    def get(refs, s):
        return refs[0][s], refs[1][s]

    def exchange(phase, value, level):
        buf = ex.at[phase]
        mine, steps, peer_of, count = (
            (inner, inner_steps, lambda t: inner_peer(*t), span)
            if level == 0
            else (outer, outer_steps, outer_peer, spans)
        )
        buf[mine] = value
        coming = []
        for n, t in reversed(list(enumerate(steps))):
            sems = ex_send.at[phase], ex_recv.at[phase, n]
            remote(buf.at[mine], buf.at[mine], *sems, peer_of(t)).start()
            origin = at_inner(-t[0], -t[1]) if level == 0 else at_outer(-t)
            coming.append((origin, remote(buf.at[origin], buf.at[origin], *sems, sibling)))
        every = buf.at[pl.ds(0, count - 1)]
        sends.append(remote(every, every, ex_send.at[phase], ex_recv.at[phase, 0], sibling))
        return phase, mine, value, coming[::-1]

    def collect(exchanged, refs, nt):
        phase, mine, value, coming = exchanged
        result = few(stacked(value), *get(refs, mine), nt)
        for origin, copy in coming:
            copy.wait_recv()
            arrived = ex[phase, origin]
            value = value + arrived
            result += few(stacked(arrived), *get(refs, origin), nt)
        return result, value

    def again(exchanged, refs, nt):
        phase, mine, value, coming = exchanged
        result = few(stacked(value), *get(refs, mine), nt)
        for origin, _ in coming:
            result += few(stacked(ex[phase, origin]), *get(refs, origin), nt)
        return result

    tail = WIDE - RIM

    def forward_local(phase, source, sums):
        vs = stacked(source)
        rim = few(vs, xh[tail:, RIM:], xl[tail:, RIM:], True)
        near = exchange(phase, with_sum(rim, sums), 0)
        parts = []
        for i in range(3):
            a, b = i * RIM, (i + 1) * RIM
            parts.append(few(vs[:, :b], xh[a:b, RIM : RIM + b], xl[a:b, RIM : RIM + b], True))
        return near, jnp.concatenate(parts + [rim], axis=1)

    def pick(value, n):
        return lane_sum(jnp.where(lane == BLK + n, value, 0.0))

    def forward_across(phase, near, local, old=None):
        value, sums = collect(near, r_refs, True)
        far = exchange(phase + 1, with_sum(value, pick(sums, 0)), 1)
        entering = again(near, m_refs, True)
        local = local - few(stacked(entering), xh[:, :RIM], xl[:, :RIM], True)
        rim = few(stacked(local), xh[:, :RIM], xl[:, :RIM], False)
        value = with_sum(rim, 0.0)
        if old is not None:
            for n, (a, b) in enumerate(((old, old), (old, local), (local, local))):
                value = jnp.where(lane == BLK + n, lane_sum(a * b), value)
        return far, local, exchange(phase + 2, value, 0)

    def backward_inside(back):
        value, received = collect(back, p_refs, False)
        return value, again(back, n_refs, False), received

    def forward_last(far, local, falling):
        value, sums = collect(far, m2_refs, True)
        vs = stacked(value)
        local = local - few(vs, wh[...], wl[...], True)
        spanned = falling[0] - few(vs, *get(t_refs, 0), False)
        own = falling[1] - few(vs, *get(t_refs, 1), False)
        return (local, spanned, own), pick(sums, 0), value

    def backward(phase, state, beside=None, part=None):
        source, spanned, own = state
        sums = lane_sum(source * source) if part is None else part
        far = exchange(phase + 3, with_sum(spanned, sums), 1)
        vs = stacked(source)
        parts = []
        for i in range(4):
            a, b = i * RIM, (i + 1) * RIM
            parts.append(
                few(vs[:, a:], xh[a:, RIM + a : RIM + b], xl[a:, RIM + a : RIM + b], False)
            )
        local = jnp.concatenate(parts, axis=1)
        if beside is not None:
            beside()
        value, sums = collect(far, n2_refs, False)
        energy = pick(sums, 0)
        if part is None:
            energy = exchange(phase + 4, jnp.where(lane == BLK, energy, 0.0), 0)
        moved = few(stacked(own + value), xh[tail:, RIM:], xl[tail:, RIM:], False)
        return local - moved, energy

    def total_of(exchanged):
        phase, _, value, coming = exchanged
        for origin, copy in coming:
            copy.wait_recv()
            value = value + ex[phase, origin]
        return pick(value, 0)

    def system_times(step, vector):
        vs = stacked(vector)
        falling = few(vs, lh[:, :RIM], ll[:, :RIM], False)
        copies = []

        def pass_on(way, value, peer):
            nbs[step, way] = value
            copy = remote(
                nbs.at[step, way], nbr.at[step, way],
                nb_send.at[step, way], nb_recv.at[step, way], peer,
            )
            copy.start()
            copies.append(copy)
            sends.append(copy)

        pass_on(0, falling, down)
        last = vector[:, tail:] + few(
            vs[:, tail:], lh[tail:, RIM + tail :], ll[tail:, RIM + tail :], False
        )
        pass_on(1, last, up)
        parts = []
        for i in range(3):
            a, b = i * RIM, (i + 1) * RIM
            parts.append(
                vector[:, a:b]
                + few(vs[:, a:], lh[a:, RIM + a : RIM + b], ll[a:, RIM + a : RIM + b], False)
            )
        upper = jnp.concatenate(parts + [last], axis=1)
        us = stacked(upper)
        parts = []
        for i in range(4):
            a, b = i * RIM, (i + 1) * RIM
            parts.append(few(us[:, :b], lh[a:b, RIM : RIM + b], ll[a:b, RIM : RIM + b], True))
        diagonal = [
            few(vs[:, i * PAD : (i + 1) * PAD], dh[i], dl[i], False) for i in range(ROWS)
        ]
        image = upper + jnp.concatenate(parts, axis=1) + jnp.concatenate(diagonal, axis=1)
        copies[0].wait_recv()
        coming = nbr[step, 0] * flag(row < total - 1)
        corner = coming + few(
            stacked(coming), lh[tail:, RIM + tail :], ll[tail:, RIM + tail :], True
        )
        copies[1].wait_recv()
        before = (nbr[step, 1] + falling) * flag(row > 0)
        image = image + few(stacked(before), lh[:, :RIM], ll[:, :RIM], True)
        return jnp.concatenate([image[:, :tail], image[:, tail:] + corner], axis=1)

    gap = jnp.zeros((columns, PAD - BLK), F32)
    residual = jnp.concatenate(
        [part for i in range(ROWS) for part in (rhs_ref[i], gap)], axis=1
    )
    near, local = forward_local(0, residual, jnp.zeros((columns, 1), F32))

    for t in range(1, cols):
        remote(
            sysl_ref, gathered.at[col], col_send, col_recv, (row, (col + t) % cols)
        ).start()
    others = gathered.at[pl.ds(0, cols - 1)]
    col_every = remote(others, others, col_send, col_recv, up)
    sends.append(col_every)
    own_copy = pltpu.make_async_copy(sysl_ref, gathered.at[col], own_sem)
    own_copy.start()

    def place_system():
        own_copy.wait()
        col_every.wait_recv()
        place(lambda i, k: gathered[k // share, i, k % share])
        for i in range(ROWS):
            high, low = split(dense[i * PAD : (i + 1) * PAD, :])
            lh[i * PAD : (i + 1) * PAD, :] = high
            ll[i * PAD : (i + 1) * PAD, :] = low
            high, low = split(padded(sysd_ref[i]))
            dh[i] = high
            dl[i] = low

    r_iota = lax.broadcasted_iota(jnp.int32, (RIM, RIM), 0)
    c_iota = lax.broadcasted_iota(jnp.int32, (RIM, RIM), 1)
    eye = jnp.where((r_iota == c_iota) & (c_iota % PAD < BLK), 1.0, 0.0).astype(F32)

    def put(refs, s, value):
        high, low = split(value)
        refs[0][s] = high
        refs[1][s] = low

    a_refs, m_refs, r_refs, n_refs, p_refs = (ah, al), (mh, ml), (rh, rl), (nh, nl), (ph, pq)
    m2_refs, n2_refs, t_refs = (m2h, m2l), (n2h, n2l), (th, tl)

    def flag(condition):
        return jnp.where(condition, 1.0, 0.0).astype(F32)

    def take_in(buf, s):
        put(a_refs, s, jnp.concatenate([unpack(buf[s, 0]), unpack(buf[s, 1])], axis=0))

    edge = xh[:, :RIM].astype(F32) + xl[:, :RIM].astype(F32)
    square = many(split(edge.T), (xh[:, :RIM], xl[:, :RIM]))
    qbuf[inner, 0] = pack(square[:BLK])
    qbuf[inner, 1] = pack(square[PAD : PAD + BLK])

    take(abuf, a_send, a_recv, functools.partial(take_in, abuf))

    level = [get(a_refs, s) for s in range(span)]
    while len(level) > 2:
        level = [split(many(level[n + 1], level[n])) for n in range(0, len(level), 2)]
    across = many(level[1], level[0])
    bbuf[outer, 0] = pack(across[:BLK])
    bbuf[outer, 1] = pack(across[PAD : PAD + BLK])
    for t in reversed(outer_steps):
        hand(bbuf, (outer, core), t, b_send, b_recv, outer_peer(t))

    give(qbuf, q_send, q_recv)

    put(m_refs, span - 1, jnp.zeros((RIM, RIM), F32))
    put(r_refs, span - 1, eye)
    put(n_refs, 0, jnp.zeros((RIM, RIM), F32))
    put(p_refs, 0, eye)

    def chain(t, carry):
        s = span - 1 - t
        right = get(a_refs, s)
        put(m_refs, s - 1, many(get(m_refs, s), right) + flag(s == inner) * eye)
        put(r_refs, s - 1, many(get(r_refs, s), right))
        left = get(a_refs, t)
        put(n_refs, t + 1, many(left, get(n_refs, t)) + flag(t == inner) * eye)
        put(p_refs, t + 1, many(left, get(p_refs, t)))
        return carry

    lax.fori_loop(0, span - 1, chain, 0)

    far, local, back = forward_across(0, near, local)

    take(qbuf, q_send, q_recv, lambda s: None)
    halves = []
    for s in range(span):
        whole = jnp.concatenate([unpack(qbuf[s, 0]), unpack(qbuf[s, 1])], axis=0)
        halves.append(split(many(split(whole), get(p_refs, s)).T))
    entered = [
        sum(many(halves[s], get(refs, s)) for s in range(span)) for refs in (p_refs, n_refs)
    ]
    put(t_refs, 0, entered[0])
    put(t_refs, 1, entered[1])
    high, low = split(many((xh[:, :RIM], xl[:, :RIM]), get(p_refs, inner)))
    wh[...] = high
    wl[...] = low

    for t in outer_steps:
        origin = at_outer(-t)
        awaited(bbuf, (origin, core), t, b_send, b_recv)
        hand(bbuf, (origin, core), spans + t, b_send, b_recv, sibling)
    falling = backward_inside(back)
    take_in(bbuf, outer)
    for t in outer_steps:
        origin = at_outer(-t)
        awaited(bbuf, (origin, 1 - core), spans + t, b_send, b_recv)
        take_in(bbuf, origin)
    mine_r = rh[inner].astype(F32) + rl[inner].astype(F32)
    put(m2_refs, spans - 1, jnp.zeros((RIM, RIM), F32))
    put(n2_refs, 0, jnp.zeros((RIM, RIM), F32))

    def outer_chain(t, carry):
        s = spans - 1 - t
        put(m2_refs, s - 1, many(get(m2_refs, s), get(a_refs, s)) + flag(s == outer) * eye)
        put(n2_refs, t + 1, many(get(a_refs, t), get(n2_refs, t)) + flag(t == outer) * mine_r)
        return carry

    lax.fori_loop(0, spans - 1, outer_chain, 0)

    state, _, _ = forward_last(far, local, falling)
    direction, waiting = backward(0, state, place_system)
    image = system_times(0, direction)
    energy = total_of(waiting)
    answer = jnp.zeros_like(residual)
    for step in range(ITERS):
        phase = 5 * (step + 1)
        near, local = forward_local(phase, image, lane_sum(direction * image))
        last = step == ITERS - 1
        far, local, back = forward_across(phase, near, local, state[0] if last else None)
        falling = backward_inside(back)
        change, curvature, entering = forward_last(far, local, falling)
        alpha = energy / curvature
        part = None
        if last:
            received = falling[2]
            crossed = pick(received, 1) - lane_sum(state[1] * entering)
            squared = pick(received, 2) - lane_sum((falling[0] + change[1]) * entering)
            part = pick(received, 0) - alpha * (2.0 * crossed - alpha * squared)
        state = tuple(old - alpha * new for old, new in zip(state, change))
        precond, waiting = backward(phase, state, part=part)
        answer = answer + alpha * direction
        residual = residual - alpha * image
        if not last:
            following = system_times(step + 1, precond)
        energy_next = waiting if last else total_of(waiting)
        ratio = energy_next / energy
        direction = precond + ratio * direction
        if not last:
            image = following + ratio * image
        energy = energy_next

    for i in range(ROWS):
        lanes = slice(i * PAD, (i + 1) * PAD)
        out_ref[0, i] = answer[:, lanes]
        out_ref[1, i] = residual[:, lanes]
        out_ref[2, i] = direction[:, lanes]
    for copy in sends:
        copy.wait_send()


def per_device(
    spans, cols, rhs, system_lower, system_diag, factor_lower, diag_inverse, neighbours, counts
):
    rows, width, columns = rhs.shape
    vmem = pl.BlockSpec(memory_space=pltpu.VMEM)
    phases = 5 * (ITERS + 1) - 1
    half = lambda: pltpu.VMEM((GROUP, RIM, RIM), BF16)
    most = max(GROUP, spans)
    tall = lambda: pltpu.VMEM((most, RIM, RIM), BF16)
    dma = pltpu.SemaphoreType.DMA
    outs = pl.pallas_call(
        functools.partial(kernel, GROUP, spans, cols),
        out_shape=jax.ShapeDtypeStruct((3, rows, columns, PAD), F32),
        in_specs=[pl.BlockSpec(memory_space=pltpu.SMEM)] * 2
        + [vmem, pl.BlockSpec(memory_space=pl.ANY)]
        + [vmem] * 3,
        out_specs=vmem,
        scratch_shapes=[
            pltpu.VMEM((WIDE, RIM + WIDE), F32),
            pltpu.VMEM((WIDE, RIM + WIDE), BF16),
            pltpu.VMEM((WIDE, RIM + WIDE), BF16),
            pltpu.VMEM((WIDE, RIM + WIDE), BF16),
            pltpu.VMEM((WIDE, RIM + WIDE), BF16),
            pltpu.VMEM((ROWS, PAD, PAD), BF16),
            pltpu.VMEM((ROWS, PAD, PAD), BF16),
            pltpu.VMEM((cols,) + system_lower.shape, F32),
            pltpu.VMEM((GROUP, 2, PACKED, PAD), F32),
            pltpu.VMEM((spans, 2, PACKED, PAD), F32),
            pltpu.VMEM((GROUP, 2, PACKED, PAD), F32),
            tall(), tall(),
            pltpu.VMEM((2, RIM, RIM), BF16), pltpu.VMEM((2, RIM, RIM), BF16),
            pltpu.VMEM((WIDE, RIM), BF16), pltpu.VMEM((WIDE, RIM), BF16),
            half(), half(), half(), half(), half(), half(), half(), half(),
            tall(), tall(), tall(), tall(),
            pltpu.VMEM((phases, most, columns, RIM), F32),
            pltpu.VMEM((ITERS, 2, columns, RIM), F32),
            pltpu.VMEM((ITERS, 2, columns, RIM), F32),
            dma, dma, dma, dma((GROUP,)), dma((GROUP,)), dma((2 * spans,)), dma((2 * spans,)),
            dma((GROUP,)), dma((GROUP,)),
            dma((phases,)), dma((phases, most - 1)), dma((ITERS, 2)), dma((ITERS, 2)),
        ],
        compiler_params=pltpu.CompilerParams(
            collective_id=0, has_side_effects=True, vmem_limit_bytes=60 * 1024 * 1024
        ),
    )(
        neighbours, counts, jnp.transpose(rhs, (0, 2, 1)), system_lower, system_diag,
        factor_lower, diag_inverse,
    )
    return tuple(jnp.transpose(outs[n, :, :, :width], (0, 2, 1)) for n in range(3))


def solution(mesh):
    in_specs = (
        P("row", None, "col"),
        P("row", "col", None, None),
        P("row", None, None),
        P("row", None, None, None),
        P("row", None, None),
        P("row", None),
        P("row"),
    )
    out_specs = (P("row", None, "col"), P("row", None, "col"), P("row", None, "col"))
    return jax.shard_map(
        functools.partial(per_device, mesh.shape["row"] // GROUP, mesh.shape["col"]),
        mesh=mesh, in_specs=in_specs, out_specs=out_specs, check_vma=False,
    )
```

```python
import functools

import jax
import jax.numpy as jnp
from jax import lax
from jax.experimental import pallas as pl
from jax.experimental.pallas import tpu as pltpu
from jax.sharding import PartitionSpec as P

ITERS = 2
GROUP = 8
BLK = 72
ROWS = 8
PAD = 128
WIDE = ROWS * PAD
RIM = 2 * PAD
PACKED = BLK + 16
F32 = jnp.float32
BF16 = jnp.bfloat16
MESH = pl.DeviceIdType.MESH


def split(x):
    high = x.astype(BF16)
    return high, (x - high.astype(F32)).astype(BF16)


def dot(a, b, nt):
    return lax.dot_general(
        a, b, (((1,), (1 if nt else 0,)), ((), ())), preferred_element_type=F32
    )


def stacked(v):
    high, low = split(v)
    return jnp.concatenate([high, low], axis=0)


def few(vs, high, low, nt):
    rows = vs.shape[0] // 2
    both = dot(vs, high, nt)
    return both[:rows] + both[rows:] + dot(vs[:rows], low, nt)


def many(a, b, nt=False):
    return dot(a[0], b[0], nt) + (dot(a[0], b[1], nt) + dot(a[1], b[0], nt))


def nearest(count):
    return sorted(range(1, count), key=lambda t: min(t, count - t))


def pack(half):
    lane = lax.broadcasted_iota(jnp.int32, (BLK, PAD), 1)
    turned = pltpu.roll(half[:, PAD:], BLK, 1)
    top = jnp.where(lane < BLK, half[:, :PAD], turned)
    rest = jnp.where(lane < 16, turned, 0.0)
    first = rest[:8]
    for g in range(1, 8):
        first += pltpu.roll(rest[8 * g : 8 * g + 8], 16 * g, 1)
    return jnp.concatenate([top, first, rest[64:]], axis=0)


def unpack(packed):
    lane = lax.broadcasted_iota(jnp.int32, (BLK, PAD), 1)
    top, first, last = packed[:BLK], packed[BLK : BLK + 8], packed[BLK + 8 :]
    edge = PAD - BLK
    rest = [pltpu.roll(first, (edge - 16 * g) % PAD, 1) for g in range(8)]
    rest = jnp.concatenate(rest + [pltpu.roll(last, edge, 1)], axis=0)
    right = jnp.where(lane < edge, pltpu.roll(top, edge, 1), jnp.where(lane < BLK, rest, 0.0))
    left = jnp.where(lane < BLK, top, 0.0)
    value = jnp.concatenate([left, right], axis=1)
    return jnp.concatenate([value, jnp.zeros((PAD - BLK, RIM), F32)], axis=0)


def kernel(
    span, spans, cols, neighbours_ref, counts_ref, rhs_ref, sysl_ref, sysd_ref, fac_ref, dinv_ref,
    out_ref,
    dense, xh, xl, lh, ll, dh, dl, gathered, abuf, bbuf, qbuf, ah, al, th, tl, wh, wl,
    mh, ml, rh, rl, nh, nl, ph, pq, m2h, m2l, n2h, n2l, ex, nbs, nbr,
    own_sem, col_send, col_recv, a_send, a_recv, b_send, b_recv, q_send, q_recv, ex_send, ex_recv, nb_send, nb_recv,
):
    row, col = lax.axis_index("row"), lax.axis_index("col")
    total = span * spans
    outer, inner = row // span, row % span
    share = sysl_ref.shape[1]
    columns = rhs_ref.shape[1]
    chips = span // 2
    chip, core = inner // 2, inner % 2

    def at_inner(x, c):
        return ((chip + x + chips) % chips) * 2 + (core + c + 2) % 2

    def at_outer(t):
        return (outer + t + spans) % spans

    def inner_peer(x, c):
        return (outer * span + at_inner(x, c), col)

    def outer_peer(t):
        return (at_outer(t) * span + inner, col)

    inner_steps = [(x, c) for x in [0] + nearest(chips) for c in range(2)][1:]
    outer_steps = nearest(spans)
    up, down = ((row + 1) % total, col), ((row + total - 1) % total, col)
    sibling = inner_peer(0, 1)

    barrier = pltpu.get_barrier_semaphore()
    greeted = (
        [inner_peer(*t) for t in inner_steps]
        + [outer_peer(t) for t in outer_steps]
        + [(row, (col + t) % cols) for t in range(1, cols)]
        + [up, down]
    )
    for peer in greeted:
        pl.semaphore_signal(barrier, inc=1, device_id=peer, device_id_type=MESH)

    sends = []

    def remote(source, target, send_sem, recv_sem, peer):
        return pltpu.make_async_remote_copy(
            src_ref=source, dst_ref=target, send_sem=send_sem, recv_sem=recv_sem,
            device_id=peer, device_id_type=MESH,
        )

    def place(block_of):
        def one(i, carry):
            blocks = [block_of(i, k) for k in range(8)]
            at = pl.multiple_of(i * PAD, PAD)
            places = [
                jnp.where(k < counts_ref[i], neighbours_ref[i, k] - row * ROWS + 2, -1)
                for k in range(8)
            ]
            for s in range(ROWS + 2):
                value = jnp.where(places[0] == s, 1.0, 0.0) * blocks[0]
                for k in range(1, 8):
                    value += jnp.where(places[k] == s, 1.0, 0.0) * blocks[k]
                dense[pl.ds(at, BLK), s * PAD : s * PAD + BLK] = value
            return carry

        lax.fori_loop(0, ROWS, one, 0)

    def padded(block):
        wide = jnp.concatenate([block, jnp.zeros((BLK, PAD - BLK), F32)], axis=1)
        return jnp.concatenate([wide, jnp.zeros((PAD - BLK, PAD), F32)], axis=0)

    dense[...] = jnp.zeros_like(dense)
    place(lambda i, k: fac_ref[i, k])

    inverses = [padded(dinv_ref[i]) for i in range(ROWS)]
    scaled = [
        many(split(inverses[i]), split(dense[i * PAD : (i + 1) * PAD, : RIM + i * PAD]))
        for i in range(ROWS)
    ]
    nothing = jnp.zeros((PAD, PAD), F32)
    for i in range(0, ROWS, 2):
        width = RIM + i * PAD
        first, second = scaled[i], scaled[i + 1][:, :width]
        taken = many(
            split(scaled[i + 1][:, width:]),
            split(jnp.concatenate([first, inverses[i]], axis=1)),
        )
        rows = jnp.concatenate([first, second - taken[:, :width]], axis=0)
        corner = jnp.concatenate(
            [
                jnp.concatenate([inverses[i], nothing], axis=1),
                jnp.concatenate([-taken[:, width:], inverses[i + 1]], axis=1),
            ],
            axis=0,
        )
        edge = rows[:, :RIM]
        if i > 0:
            step = many(split(rows[:, RIM:]), (xh[: i * PAD, :width], xl[: i * PAD, :width]))
            edge = edge - step[:, :RIM]
            body = [edge, -step[:, RIM:], corner]
        else:
            body = [edge, corner]
        if i < ROWS - 2:
            body.append(jnp.zeros((2 * PAD, WIDE - (i + 2) * PAD), F32))
        high, low = split(jnp.concatenate(body, axis=1))
        xh[i * PAD : (i + 2) * PAD, :] = high
        xl[i * PAD : (i + 2) * PAD, :] = low
    abuf[inner, 0] = pack(-edge[:BLK, :])
    abuf[inner, 1] = pack(-edge[PAD : PAD + BLK, :])

    pl.semaphore_wait(barrier, len(greeted))

    def hand(buf, slot, n, send, recv, peer):
        copy = remote(buf.at[slot], buf.at[slot], send.at[n], recv.at[n], peer)
        copy.start()
        sends.append(copy)

    def awaited(buf, slot, n, send, recv):
        remote(buf.at[slot], buf.at[slot], send.at[n], recv.at[n], sibling).wait_recv()

    def give(buf, send, recv):
        for x in reversed(nearest(chips)):
            hand(buf, inner, x, send, recv, inner_peer(x, 0))
        hand(buf, inner, 0, send, recv, sibling)

    def take(buf, send, recv, use):
        use(inner)
        awaited(buf, at_inner(0, 1), 0, send, recv)
        use(at_inner(0, 1))
        for x in nearest(chips):
            origin = at_inner(-x, 0)
            awaited(buf, origin, x, send, recv)
            hand(buf, origin, chips + x, send, recv, sibling)
            use(origin)
        for x in nearest(chips):
            origin = at_inner(-x, 1)
            awaited(buf, origin, chips + x, send, recv)
            use(origin)

    give(abuf, a_send, a_recv)

    lane = lax.broadcasted_iota(jnp.int32, (columns, RIM), 1)

    def with_sum(value, sums):
        return jnp.where(lane == BLK, sums, jnp.where(lane % PAD < BLK, value, 0.0))

    def lane_sum(value):
        return jnp.sum(value, axis=1, keepdims=True)

    def get(refs, s):
        return refs[0][s], refs[1][s]

    def exchange(phase, value, level):
        buf = ex.at[phase]
        mine, steps, peer_of, count = (
            (inner, inner_steps, lambda t: inner_peer(*t), span)
            if level == 0
            else (outer, outer_steps, outer_peer, spans)
        )
        buf[mine] = value
        coming = []
        for n, t in reversed(list(enumerate(steps))):
            sems = ex_send.at[phase], ex_recv.at[phase, n]
            remote(buf.at[mine], buf.at[mine], *sems, peer_of(t)).start()
            origin = at_inner(-t[0], -t[1]) if level == 0 else at_outer(-t)
            coming.append((origin, remote(buf.at[origin], buf.at[origin], *sems, sibling)))
        every = buf.at[pl.ds(0, count - 1)]
        sends.append(remote(every, every, ex_send.at[phase], ex_recv.at[phase, 0], sibling))
        return phase, mine, value, coming[::-1]

    def collect(exchanged, refs, nt):
        phase, mine, value, coming = exchanged
        result = few(stacked(value), *get(refs, mine), nt)
        for origin, copy in coming:
            copy.wait_recv()
            arrived = ex[phase, origin]
            value = value + arrived
            result += few(stacked(arrived), *get(refs, origin), nt)
        return result, value

    def again(exchanged, refs, nt):
        phase, mine, value, coming = exchanged
        result = few(stacked(value), *get(refs, mine), nt)
        for origin, _ in coming:
            result += few(stacked(ex[phase, origin]), *get(refs, origin), nt)
        return result

    tail = WIDE - RIM

    def forward_local(phase, source, sums):
        vs = stacked(source)
        rim = few(vs, xh[tail:, RIM:], xl[tail:, RIM:], True)
        near = exchange(phase, with_sum(rim, sums), 0)
        parts = []
        for i in range(3):
            a, b = i * RIM, (i + 1) * RIM
            parts.append(few(vs[:, :b], xh[a:b, RIM : RIM + b], xl[a:b, RIM : RIM + b], True))
        return near, jnp.concatenate(parts + [rim], axis=1)

    def pick(value, n):
        return lane_sum(jnp.where(lane == BLK + n, value, 0.0))

    def forward_across(phase, near, local, old=None):
        value, sums = collect(near, r_refs, True)
        far = exchange(phase + 1, with_sum(value, pick(sums, 0)), 1)
        entering = again(near, m_refs, True)
        local = local - few(stacked(entering), xh[:, :RIM], xl[:, :RIM], True)
        rim = few(stacked(local), xh[:, :RIM], xl[:, :RIM], False)
        value = with_sum(rim, 0.0)
        if old is not None:
            for n, (a, b) in enumerate(((old, old), (old, local), (local, local))):
                value = jnp.where(lane == BLK + n, lane_sum(a * b), value)
        return far, local, exchange(phase + 2, value, 0)

    def backward_inside(back):
        value, received = collect(back, p_refs, False)
        return value, again(back, n_refs, False), received

    def forward_last(far, local, falling):
        value, sums = collect(far, m2_refs, True)
        vs = stacked(value)
        local = local - few(vs, wh[...], wl[...], True)
        spanned = falling[0] - few(vs, *get(t_refs, 0), False)
        own = falling[1] - few(vs, *get(t_refs, 1), False)
        return (local, spanned, own), pick(sums, 0), value

    def backward(phase, state, beside=None, part=None):
        source, spanned, own = state
        sums = lane_sum(source * source) if part is None else part
        far = exchange(phase + 3, with_sum(spanned, sums), 1)
        vs = stacked(source)
        parts = []
        for i in range(4):
            a, b = i * RIM, (i + 1) * RIM
            parts.append(
                few(vs[:, a:], xh[a:, RIM + a : RIM + b], xl[a:, RIM + a : RIM + b], False)
            )
        local = jnp.concatenate(parts, axis=1)
        if beside is not None:
            beside()
        value, sums = collect(far, n2_refs, False)
        energy = pick(sums, 0)
        if part is None:
            energy = exchange(phase + 4, jnp.where(lane == BLK, energy, 0.0), 0)
        moved = few(stacked(own + value), xh[tail:, RIM:], xl[tail:, RIM:], False)
        return local - moved, energy

    def total_of(exchanged):
        phase, _, value, coming = exchanged
        for origin, copy in coming:
            copy.wait_recv()
            value = value + ex[phase, origin]
        return pick(value, 0)

    def system_times(step, vector):
        vs = stacked(vector)
        falling = few(vs, lh[:, :RIM], ll[:, :RIM], False)
        copies = []

        def pass_on(way, value, peer):
            nbs[step, way] = value
            copy = remote(
                nbs.at[step, way], nbr.at[step, way],
                nb_send.at[step, way], nb_recv.at[step, way], peer,
            )
            copy.start()
            copies.append(copy)
            sends.append(copy)

        pass_on(0, falling, down)
        last = vector[:, tail:] + few(
            vs[:, tail:], lh[tail:, RIM + tail :], ll[tail:, RIM + tail :], False
        )
        pass_on(1, last, up)
        parts = []
        for i in range(3):
            a, b = i * RIM, (i + 1) * RIM
            parts.append(
                vector[:, a:b]
                + few(vs[:, a:], lh[a:, RIM + a : RIM + b], ll[a:, RIM + a : RIM + b], False)
            )
        upper = jnp.concatenate(parts + [last], axis=1)
        us = stacked(upper)
        parts = []
        for i in range(4):
            a, b = i * RIM, (i + 1) * RIM
            parts.append(few(us[:, :b], lh[a:b, RIM : RIM + b], ll[a:b, RIM : RIM + b], True))
        diagonal = [
            few(vs[:, i * PAD : (i + 1) * PAD], dh[i], dl[i], False) for i in range(ROWS)
        ]
        image = upper + jnp.concatenate(parts, axis=1) + jnp.concatenate(diagonal, axis=1)
        copies[0].wait_recv()
        coming = nbr[step, 0] * flag(row < total - 1)
        corner = coming + few(
            stacked(coming), lh[tail:, RIM + tail :], ll[tail:, RIM + tail :], True
        )
        copies[1].wait_recv()
        before = (nbr[step, 1] + falling) * flag(row > 0)
        image = image + few(stacked(before), lh[:, :RIM], ll[:, :RIM], True)
        return jnp.concatenate([image[:, :tail], image[:, tail:] + corner], axis=1)

    gap = jnp.zeros((columns, PAD - BLK), F32)
    residual = jnp.concatenate(
        [part for i in range(ROWS) for part in (rhs_ref[i], gap)], axis=1
    )
    near, local = forward_local(0, residual, jnp.zeros((columns, 1), F32))

    for t in range(1, cols):
        remote(
            sysl_ref, gathered.at[col], col_send, col_recv, (row, (col + t) % cols)
        ).start()
    others = gathered.at[pl.ds(0, cols - 1)]
    col_every = remote(others, others, col_send, col_recv, up)
    sends.append(col_every)
    own_copy = pltpu.make_async_copy(sysl_ref, gathered.at[col], own_sem)
    own_copy.start()

    def place_system():
        own_copy.wait()
        col_every.wait_recv()
        place(lambda i, k: gathered[k // share, i, k % share])
        for i in range(ROWS):
            high, low = split(dense[i * PAD : (i + 1) * PAD, :])
            lh[i * PAD : (i + 1) * PAD, :] = high
            ll[i * PAD : (i + 1) * PAD, :] = low
            high, low = split(padded(sysd_ref[i]))
            dh[i] = high
            dl[i] = low

    r_iota = lax.broadcasted_iota(jnp.int32, (RIM, RIM), 0)
    c_iota = lax.broadcasted_iota(jnp.int32, (RIM, RIM), 1)
    eye = jnp.where((r_iota == c_iota) & (c_iota % PAD < BLK), 1.0, 0.0).astype(F32)

    def put(refs, s, value):
        high, low = split(value)
        refs[0][s] = high
        refs[1][s] = low

    a_refs, m_refs, r_refs, n_refs, p_refs = (ah, al), (mh, ml), (rh, rl), (nh, nl), (ph, pq)
    m2_refs, n2_refs, t_refs = (m2h, m2l), (n2h, n2l), (th, tl)

    def flag(condition):
        return jnp.where(condition, 1.0, 0.0).astype(F32)

    def take_in(buf, s):
        put(a_refs, s, jnp.concatenate([unpack(buf[s, 0]), unpack(buf[s, 1])], axis=0))

    edge = xh[:, :RIM].astype(F32) + xl[:, :RIM].astype(F32)
    square = many(split(edge.T), (xh[:, :RIM], xl[:, :RIM]))
    qbuf[inner, 0] = pack(square[:BLK])
    qbuf[inner, 1] = pack(square[PAD : PAD + BLK])

    take(abuf, a_send, a_recv, functools.partial(take_in, abuf))

    level = [get(a_refs, s) for s in range(span)]
    while len(level) > 2:
        level = [split(many(level[n + 1], level[n])) for n in range(0, len(level), 2)]
    across = many(level[1], level[0])
    bbuf[outer, 0] = pack(across[:BLK])
    bbuf[outer, 1] = pack(across[PAD : PAD + BLK])
    for t in reversed(outer_steps):
        hand(bbuf, (outer, core), t, b_send, b_recv, outer_peer(t))

    give(qbuf, q_send, q_recv)

    put(m_refs, span - 1, jnp.zeros((RIM, RIM), F32))
    put(r_refs, span - 1, eye)
    put(n_refs, 0, jnp.zeros((RIM, RIM), F32))
    put(p_refs, 0, eye)

    def chain(t, carry):
        s = span - 1 - t
        right = get(a_refs, s)
        put(m_refs, s - 1, many(get(m_refs, s), right) + flag(s == inner) * eye)
        put(r_refs, s - 1, many(get(r_refs, s), right))
        left = get(a_refs, t)
        put(n_refs, t + 1, many(left, get(n_refs, t)) + flag(t == inner) * eye)
        put(p_refs, t + 1, many(left, get(p_refs, t)))
        return carry

    lax.fori_loop(0, span - 1, chain, 0)

    far, local, back = forward_across(0, near, local)

    take(qbuf, q_send, q_recv, lambda s: None)
    halves = []
    for s in range(span):
        whole = jnp.concatenate([unpack(qbuf[s, 0]), unpack(qbuf[s, 1])], axis=0)
        halves.append(split(many(split(whole), get(p_refs, s)).T))
    entered = [
        sum(many(halves[s], get(refs, s)) for s in range(span)) for refs in (p_refs, n_refs)
    ]
    put(t_refs, 0, entered[0])
    put(t_refs, 1, entered[1])
    high, low = split(many((xh[:, :RIM], xl[:, :RIM]), get(p_refs, inner)))
    wh[...] = high
    wl[...] = low

    for t in outer_steps:
        origin = at_outer(-t)
        awaited(bbuf, (origin, core), t, b_send, b_recv)
        hand(bbuf, (origin, core), spans + t, b_send, b_recv, sibling)
    falling = backward_inside(back)
    take_in(bbuf, outer)
    for t in outer_steps:
        origin = at_outer(-t)
        awaited(bbuf, (origin, 1 - core), spans + t, b_send, b_recv)
        take_in(bbuf, origin)
    mine_r = rh[inner].astype(F32) + rl[inner].astype(F32)
    put(m2_refs, spans - 1, jnp.zeros((RIM, RIM), F32))
    put(n2_refs, 0, jnp.zeros((RIM, RIM), F32))

    def outer_chain(t, carry):
        s = spans - 1 - t
        put(m2_refs, s - 1, many(get(m2_refs, s), get(a_refs, s)) + flag(s == outer) * eye)
        put(n2_refs, t + 1, many(get(a_refs, t), get(n2_refs, t)) + flag(t == outer) * mine_r)
        return carry

    lax.fori_loop(0, spans - 1, outer_chain, 0, unroll=True)

    state, _, _ = forward_last(far, local, falling)
    direction, waiting = backward(0, state, place_system)
    image = system_times(0, direction)
    energy = total_of(waiting)
    answer = jnp.zeros_like(residual)

    def write(n, value):
        for i in range(ROWS):
            out_ref[n, i] = value[:, i * PAD : (i + 1) * PAD]

    for step in range(ITERS):
        phase = 5 * (step + 1)
        near, local = forward_local(phase, image, lane_sum(direction * image))
        last = step == ITERS - 1
        far, local, back = forward_across(phase, near, local, state[0] if last else None)
        falling = backward_inside(back)
        change, curvature, entering = forward_last(far, local, falling)
        alpha = energy / curvature
        part = None
        if last:
            received = falling[2]
            crossed = pick(received, 1) - lane_sum(state[1] * entering)
            squared = pick(received, 2) - lane_sum((falling[0] + change[1]) * entering)
            part = pick(received, 0) - alpha * (2.0 * crossed - alpha * squared)
        state = tuple(old - alpha * new for old, new in zip(state, change))
        held = []

        def settle():
            held.append(answer + alpha * direction)
            held.append(residual - alpha * image)
            if last:
                write(0, held[0])
                write(1, held[1])
                for copy in sends[:-1]:
                    copy.wait_send()
                del sends[:-1]

        precond, waiting = backward(phase, state, settle, part)
        answer, residual = held
        if not last:
            following = system_times(step + 1, precond)
        energy_next = waiting if last else total_of(waiting)
        ratio = energy_next / energy
        direction = precond + ratio * direction
        if not last:
            image = following + ratio * image
        energy = energy_next

    write(2, direction)
    for copy in sends:
        copy.wait_send()


def per_device(
    spans, cols, rhs, system_lower, system_diag, factor_lower, diag_inverse, neighbours, counts
):
    rows, width, columns = rhs.shape
    vmem = pl.BlockSpec(memory_space=pltpu.VMEM)
    phases = 5 * (ITERS + 1) - 1
    half = lambda: pltpu.VMEM((GROUP, RIM, RIM), BF16)
    most = max(GROUP, spans)
    tall = lambda: pltpu.VMEM((most, RIM, RIM), BF16)
    dma = pltpu.SemaphoreType.DMA
    outs = pl.pallas_call(
        functools.partial(kernel, GROUP, spans, cols),
        out_shape=jax.ShapeDtypeStruct((3, rows, columns, PAD), F32),
        in_specs=[pl.BlockSpec(memory_space=pltpu.SMEM)] * 2
        + [vmem, pl.BlockSpec(memory_space=pl.ANY)]
        + [vmem] * 3,
        out_specs=vmem,
        scratch_shapes=[
            pltpu.VMEM((WIDE, RIM + WIDE), F32),
            pltpu.VMEM((WIDE, RIM + WIDE), BF16),
            pltpu.VMEM((WIDE, RIM + WIDE), BF16),
            pltpu.VMEM((WIDE, RIM + WIDE), BF16),
            pltpu.VMEM((WIDE, RIM + WIDE), BF16),
            pltpu.VMEM((ROWS, PAD, PAD), BF16),
            pltpu.VMEM((ROWS, PAD, PAD), BF16),
            pltpu.VMEM((cols,) + system_lower.shape, F32),
            pltpu.VMEM((GROUP, 2, PACKED, PAD), F32),
            pltpu.VMEM((spans, 2, PACKED, PAD), F32),
            pltpu.VMEM((GROUP, 2, PACKED, PAD), F32),
            tall(), tall(),
            pltpu.VMEM((2, RIM, RIM), BF16), pltpu.VMEM((2, RIM, RIM), BF16),
            pltpu.VMEM((WIDE, RIM), BF16), pltpu.VMEM((WIDE, RIM), BF16),
            half(), half(), half(), half(), half(), half(), half(), half(),
            tall(), tall(), tall(), tall(),
            pltpu.VMEM((phases, most, columns, RIM), F32),
            pltpu.VMEM((ITERS, 2, columns, RIM), F32),
            pltpu.VMEM((ITERS, 2, columns, RIM), F32),
            dma, dma, dma, dma((GROUP,)), dma((GROUP,)), dma((2 * spans,)), dma((2 * spans,)),
            dma((GROUP,)), dma((GROUP,)),
            dma((phases,)), dma((phases, most - 1)), dma((ITERS, 2)), dma((ITERS, 2)),
        ],
        compiler_params=pltpu.CompilerParams(
            collective_id=0, has_side_effects=True, vmem_limit_bytes=60 * 1024 * 1024
        ),
    )(
        neighbours, counts, jnp.transpose(rhs, (0, 2, 1)), system_lower, system_diag,
        factor_lower, diag_inverse,
    )
    return tuple(jnp.transpose(outs[n, :, :, :width], (0, 2, 1)) for n in range(3))


def solution(mesh):
    in_specs = (
        P("row", None, "col"),
        P("row", "col", None, None),
        P("row", None, None),
        P("row", None, None, None),
        P("row", None, None),
        P("row", None),
        P("row"),
    )
    out_specs = (P("row", None, "col"), P("row", None, "col"), P("row", None, "col"))
    return jax.shard_map(
        functools.partial(per_device, mesh.shape["row"] // GROUP, mesh.shape["col"]),
        mesh=mesh, in_specs=in_specs, out_specs=out_specs, check_vma=False,
    )
```

```python
import functools

import jax
import jax.numpy as jnp
from jax import lax
from jax.experimental import pallas as pl
from jax.experimental.pallas import tpu as pltpu
from jax.sharding import PartitionSpec as P

ITERS = 2
GROUP = 8
BLK = 72
ROWS = 8
PAD = 128
WIDE = ROWS * PAD
RIM = 2 * PAD
PACKED = BLK + 16
F32 = jnp.float32
BF16 = jnp.bfloat16
MESH = pl.DeviceIdType.MESH


def split(x):
    high = x.astype(BF16)
    return high, (x - high.astype(F32)).astype(BF16)


def dot(a, b, nt):
    return lax.dot_general(
        a, b, (((1,), (1 if nt else 0,)), ((), ())), preferred_element_type=F32
    )


def stacked(v):
    high, low = split(v)
    return jnp.concatenate([high, low], axis=0)


def few(vs, high, low, nt):
    rows = vs.shape[0] // 2
    both = dot(vs, high, nt)
    return both[:rows] + both[rows:] + dot(vs[:rows], low, nt)


def many(a, b, nt=False):
    return dot(a[0], b[0], nt) + (dot(a[0], b[1], nt) + dot(a[1], b[0], nt))


def nearest(count):
    return sorted(range(1, count), key=lambda t: min(t, count - t))


def pack(half):
    lane = lax.broadcasted_iota(jnp.int32, (BLK, PAD), 1)
    turned = pltpu.roll(half[:, PAD:], BLK, 1)
    top = jnp.where(lane < BLK, half[:, :PAD], turned)
    rest = jnp.where(lane < 16, turned, 0.0)
    first = rest[:8]
    for g in range(1, 8):
        first += pltpu.roll(rest[8 * g : 8 * g + 8], 16 * g, 1)
    return jnp.concatenate([top, first, rest[64:]], axis=0)


def unpack(packed):
    lane = lax.broadcasted_iota(jnp.int32, (BLK, PAD), 1)
    top, first, last = packed[:BLK], packed[BLK : BLK + 8], packed[BLK + 8 :]
    edge = PAD - BLK
    rest = [pltpu.roll(first, (edge - 16 * g) % PAD, 1) for g in range(8)]
    rest = jnp.concatenate(rest + [pltpu.roll(last, edge, 1)], axis=0)
    right = jnp.where(lane < edge, pltpu.roll(top, edge, 1), jnp.where(lane < BLK, rest, 0.0))
    left = jnp.where(lane < BLK, top, 0.0)
    value = jnp.concatenate([left, right], axis=1)
    return jnp.concatenate([value, jnp.zeros((PAD - BLK, RIM), F32)], axis=0)


def kernel(
    span, spans, cols, neighbours_ref, counts_ref, rhs_ref, sysl_ref, sysd_ref, fac_ref, dinv_ref,
    out_ref,
    dense, xh, xl, lh, ll, dh, dl, gathered, abuf, bbuf, qbuf, ah, al, th, tl, wh, wl,
    mh, ml, rh, rl, nh, nl, ph, pq, m2h, m2l, n2h, n2l, ex, nbs, nbr,
    own_sem, col_send, col_recv, a_send, a_recv, b_send, b_recv, q_send, q_recv, ex_send, ex_recv, nb_send, nb_recv,
):
    row, col = lax.axis_index("row"), lax.axis_index("col")
    total = span * spans
    outer, inner = row // span, row % span
    share = sysl_ref.shape[1]
    columns = rhs_ref.shape[1]
    chips = span // 2
    chip, core = inner // 2, inner % 2

    def at_inner(x, c):
        return ((chip + x + chips) % chips) * 2 + (core + c + 2) % 2

    def at_outer(t):
        return (outer + t + spans) % spans

    def inner_peer(x, c):
        return (outer * span + at_inner(x, c), col)

    def outer_peer(t):
        return (at_outer(t) * span + inner, col)

    inner_steps = [(x, c) for x in [0] + nearest(chips) for c in range(2)][1:]
    outer_steps = nearest(spans)
    up, down = ((row + 1) % total, col), ((row + total - 1) % total, col)
    sibling = inner_peer(0, 1)

    barrier = pltpu.get_barrier_semaphore()
    greeted = (
        [inner_peer(*t) for t in inner_steps]
        + [outer_peer(t) for t in outer_steps]
        + [(row, (col + t) % cols) for t in range(1, cols)]
        + [up, down]
    )
    for peer in greeted:
        pl.semaphore_signal(barrier, inc=1, device_id=peer, device_id_type=MESH)

    sends = []

    def remote(source, target, send_sem, recv_sem, peer):
        return pltpu.make_async_remote_copy(
            src_ref=source, dst_ref=target, send_sem=send_sem, recv_sem=recv_sem,
            device_id=peer, device_id_type=MESH,
        )

    def place(block_of):
        def one(i, carry):
            blocks = [block_of(i, k) for k in range(8)]
            at = pl.multiple_of(i * PAD, PAD)
            places = [
                jnp.where(k < counts_ref[i], neighbours_ref[i, k] - row * ROWS + 2, -1)
                for k in range(8)
            ]
            for s in range(ROWS + 2):
                value = jnp.where(places[0] == s, 1.0, 0.0) * blocks[0]
                for k in range(1, 8):
                    value += jnp.where(places[k] == s, 1.0, 0.0) * blocks[k]
                dense[pl.ds(at, BLK), s * PAD : s * PAD + BLK] = value
            return carry

        lax.fori_loop(0, ROWS, one, 0)

    def padded(block):
        wide = jnp.concatenate([block, jnp.zeros((BLK, PAD - BLK), F32)], axis=1)
        return jnp.concatenate([wide, jnp.zeros((PAD - BLK, PAD), F32)], axis=0)

    dense[...] = jnp.zeros_like(dense)
    place(lambda i, k: fac_ref[i, k])

    inverses = [padded(dinv_ref[i]) for i in range(ROWS)]
    scaled = [
        many(split(inverses[i]), split(dense[i * PAD : (i + 1) * PAD, : RIM + i * PAD]))
        for i in range(ROWS)
    ]
    nothing = jnp.zeros((PAD, PAD), F32)
    for i in range(0, ROWS, 2):
        width = RIM + i * PAD
        first, second = scaled[i], scaled[i + 1][:, :width]
        taken = many(
            split(scaled[i + 1][:, width:]),
            split(jnp.concatenate([first, inverses[i]], axis=1)),
        )
        rows = jnp.concatenate([first, second - taken[:, :width]], axis=0)
        corner = jnp.concatenate(
            [
                jnp.concatenate([inverses[i], nothing], axis=1),
                jnp.concatenate([-taken[:, width:], inverses[i + 1]], axis=1),
            ],
            axis=0,
        )
        edge = rows[:, :RIM]
        if i > 0:
            step = many(split(rows[:, RIM:]), (xh[: i * PAD, :width], xl[: i * PAD, :width]))
            edge = edge - step[:, :RIM]
            body = [edge, -step[:, RIM:], corner]
        else:
            body = [edge, corner]
        if i < ROWS - 2:
            body.append(jnp.zeros((2 * PAD, WIDE - (i + 2) * PAD), F32))
        high, low = split(jnp.concatenate(body, axis=1))
        xh[i * PAD : (i + 2) * PAD, :] = high
        xl[i * PAD : (i + 2) * PAD, :] = low
    abuf[inner, 0] = pack(-edge[:BLK, :])
    abuf[inner, 1] = pack(-edge[PAD : PAD + BLK, :])

    pl.semaphore_wait(barrier, len(greeted))

    def hand(buf, slot, n, send, recv, peer):
        copy = remote(buf.at[slot], buf.at[slot], send.at[n], recv.at[n], peer)
        copy.start()
        sends.append(copy)

    def awaited(buf, slot, n, send, recv):
        remote(buf.at[slot], buf.at[slot], send.at[n], recv.at[n], sibling).wait_recv()

    def give(buf, send, recv):
        for x in reversed(nearest(chips)):
            hand(buf, inner, x, send, recv, inner_peer(x, 0))
        hand(buf, inner, 0, send, recv, sibling)

    def take(buf, send, recv, use):
        use(inner)
        awaited(buf, at_inner(0, 1), 0, send, recv)
        use(at_inner(0, 1))
        for x in nearest(chips):
            origin = at_inner(-x, 0)
            awaited(buf, origin, x, send, recv)
            hand(buf, origin, chips + x, send, recv, sibling)
            use(origin)
        for x in nearest(chips):
            origin = at_inner(-x, 1)
            awaited(buf, origin, chips + x, send, recv)
            use(origin)

    give(abuf, a_send, a_recv)

    lane = lax.broadcasted_iota(jnp.int32, (columns, RIM), 1)

    def with_sum(value, sums):
        return jnp.where(lane == BLK, sums, jnp.where(lane % PAD < BLK, value, 0.0))

    def lane_sum(value):
        return jnp.sum(value, axis=1, keepdims=True)

    def get(refs, s):
        return refs[0][s], refs[1][s]

    def exchange(phase, value, level):
        buf = ex.at[phase]
        mine, steps, peer_of, count = (
            (inner, inner_steps, lambda t: inner_peer(*t), span)
            if level == 0
            else (outer, outer_steps, outer_peer, spans)
        )
        buf[mine] = value
        coming = []
        for n, t in reversed(list(enumerate(steps))):
            sems = ex_send.at[phase], ex_recv.at[phase, n]
            remote(buf.at[mine], buf.at[mine], *sems, peer_of(t)).start()
            origin = at_inner(-t[0], -t[1]) if level == 0 else at_outer(-t)
            coming.append((origin, remote(buf.at[origin], buf.at[origin], *sems, sibling)))
        every = buf.at[pl.ds(0, count - 1)]
        sends.append(remote(every, every, ex_send.at[phase], ex_recv.at[phase, 0], sibling))
        return phase, mine, value, coming[::-1]

    def collect(exchanged, refs, nt):
        phase, mine, value, coming = exchanged
        result = few(stacked(value), *get(refs, mine), nt)
        for origin, copy in coming:
            copy.wait_recv()
            arrived = ex[phase, origin]
            value = value + arrived
            result += few(stacked(arrived), *get(refs, origin), nt)
        return result, value

    def again(exchanged, refs, nt):
        phase, mine, value, coming = exchanged
        result = few(stacked(value), *get(refs, mine), nt)
        for origin, _ in coming:
            result += few(stacked(ex[phase, origin]), *get(refs, origin), nt)
        return result

    tail = WIDE - RIM

    def forward_local(phase, source, sums):
        vs = stacked(source)
        rim = few(vs, xh[tail:, RIM:], xl[tail:, RIM:], True)
        near = exchange(phase, with_sum(rim, sums), 0)
        parts = []
        for i in range(3):
            a, b = i * RIM, (i + 1) * RIM
            parts.append(few(vs[:, :b], xh[a:b, RIM : RIM + b], xl[a:b, RIM : RIM + b], True))
        return near, jnp.concatenate(parts + [rim], axis=1)

    def pick(value, n):
        return lane_sum(jnp.where(lane == BLK + n, value, 0.0))

    def forward_across(phase, near, local, old=None):
        value, sums = collect(near, r_refs, True)
        far = exchange(phase + 1, with_sum(value, pick(sums, 0)), 1)
        entering = again(near, m_refs, True)
        local = local - few(stacked(entering), xh[:, :RIM], xl[:, :RIM], True)
        rim = few(stacked(local), xh[:, :RIM], xl[:, :RIM], False)
        value = with_sum(rim, 0.0)
        if old is not None:
            for n, (a, b) in enumerate(((old, old), (old, local), (local, local))):
                value = jnp.where(lane == BLK + n, lane_sum(a * b), value)
        return far, local, exchange(phase + 2, value, 0)

    def backward_inside(back):
        value, received = collect(back, p_refs, False)
        return value, again(back, n_refs, False), received

    def forward_last(far, local, falling):
        value, sums = collect(far, m2_refs, True)
        vs = stacked(value)
        local = local - few(vs, wh[...], wl[...], True)
        spanned = falling[0] - few(vs, *get(t_refs, 0), False)
        own = falling[1] - few(vs, *get(t_refs, 1), False)
        return (local, spanned, own), pick(sums, 0), value

    def backward(phase, state, beside=None, part=None):
        source, spanned, own = state
        sums = lane_sum(source * source) if part is None else part
        far = exchange(phase + 3, with_sum(spanned, sums), 1)
        vs = stacked(source)
        parts = []
        for i in range(4):
            a, b = i * RIM, (i + 1) * RIM
            parts.append(
                few(vs[:, a:], xh[a:, RIM + a : RIM + b], xl[a:, RIM + a : RIM + b], False)
            )
        local = jnp.concatenate(parts, axis=1)
        if beside is not None:
            beside()
        value, sums = collect(far, n2_refs, False)
        energy = pick(sums, 0)
        if part is None:
            energy = exchange(phase + 4, jnp.where(lane == BLK, energy, 0.0), 0)
        moved = few(stacked(own + value), xh[tail:, RIM:], xl[tail:, RIM:], False)
        return local - moved, energy

    def total_of(exchanged):
        phase, _, value, coming = exchanged
        for origin, copy in coming:
            copy.wait_recv()
            value = value + ex[phase, origin]
        return pick(value, 0)

    def system_times(step, vector):
        vs = stacked(vector)
        falling = few(vs, lh[:, :RIM], ll[:, :RIM], False)
        copies = []

        def pass_on(way, value, peer):
            nbs[step, way] = value
            copy = remote(
                nbs.at[step, way], nbr.at[step, way],
                nb_send.at[step, way], nb_recv.at[step, way], peer,
            )
            copy.start()
            copies.append(copy)
            sends.append(copy)

        pass_on(0, falling, down)
        last = vector[:, tail:] + few(
            vs[:, tail:], lh[tail:, RIM + tail :], ll[tail:, RIM + tail :], False
        )
        pass_on(1, last, up)
        parts = []
        for i in range(3):
            a, b = i * RIM, (i + 1) * RIM
            parts.append(
                vector[:, a:b]
                + few(vs[:, a:], lh[a:, RIM + a : RIM + b], ll[a:, RIM + a : RIM + b], False)
            )
        upper = jnp.concatenate(parts + [last], axis=1)
        us = stacked(upper)
        parts = []
        for i in range(4):
            a, b = i * RIM, (i + 1) * RIM
            parts.append(few(us[:, :b], lh[a:b, RIM : RIM + b], ll[a:b, RIM : RIM + b], True))
        diagonal = [
            few(vs[:, i * PAD : (i + 1) * PAD], dh[i], dl[i], False) for i in range(ROWS)
        ]
        image = upper + jnp.concatenate(parts, axis=1) + jnp.concatenate(diagonal, axis=1)
        copies[0].wait_recv()
        coming = nbr[step, 0] * flag(row < total - 1)
        corner = coming + few(
            stacked(coming), lh[tail:, RIM + tail :], ll[tail:, RIM + tail :], True
        )
        copies[1].wait_recv()
        before = (nbr[step, 1] + falling) * flag(row > 0)
        image = image + few(stacked(before), lh[:, :RIM], ll[:, :RIM], True)
        return jnp.concatenate([image[:, :tail], image[:, tail:] + corner], axis=1)

    gap = jnp.zeros((columns, PAD - BLK), F32)
    residual = jnp.concatenate(
        [part for i in range(ROWS) for part in (rhs_ref[i], gap)], axis=1
    )
    near, local = forward_local(0, residual, jnp.zeros((columns, 1), F32))

    for t in range(1, cols):
        remote(
            sysl_ref, gathered.at[col], col_send, col_recv, (row, (col + t) % cols)
        ).start()
    others = gathered.at[pl.ds(0, cols - 1)]
    col_every = remote(others, others, col_send, col_recv, up)
    sends.append(col_every)
    own_copy = pltpu.make_async_copy(sysl_ref, gathered.at[col], own_sem)
    own_copy.start()

    def place_system():
        own_copy.wait()
        col_every.wait_recv()
        place(lambda i, k: gathered[k // share, i, k % share])
        for i in range(ROWS):
            high, low = split(dense[i * PAD : (i + 1) * PAD, :])
            lh[i * PAD : (i + 1) * PAD, :] = high
            ll[i * PAD : (i + 1) * PAD, :] = low
            high, low = split(padded(sysd_ref[i]))
            dh[i] = high
            dl[i] = low

    r_iota = lax.broadcasted_iota(jnp.int32, (RIM, RIM), 0)
    c_iota = lax.broadcasted_iota(jnp.int32, (RIM, RIM), 1)
    eye = jnp.where((r_iota == c_iota) & (c_iota % PAD < BLK), 1.0, 0.0).astype(F32)

    def put(refs, s, value):
        high, low = split(value)
        refs[0][s] = high
        refs[1][s] = low

    a_refs, m_refs, r_refs, n_refs, p_refs = (ah, al), (mh, ml), (rh, rl), (nh, nl), (ph, pq)
    m2_refs, n2_refs, t_refs = (m2h, m2l), (n2h, n2l), (th, tl)

    def flag(condition):
        return jnp.where(condition, 1.0, 0.0).astype(F32)

    def take_in(buf, s):
        put(a_refs, s, jnp.concatenate([unpack(buf[s, 0]), unpack(buf[s, 1])], axis=0))

    edge = xh[:, :RIM].astype(F32) + xl[:, :RIM].astype(F32)
    square = many(split(edge.T), (xh[:, :RIM], xl[:, :RIM]))
    qbuf[inner, 0] = pack(square[:BLK])
    qbuf[inner, 1] = pack(square[PAD : PAD + BLK])

    take(abuf, a_send, a_recv, functools.partial(take_in, abuf))

    level = [get(a_refs, s) for s in range(span)]
    while len(level) > 2:
        level = [split(many(level[n + 1], level[n])) for n in range(0, len(level), 2)]
    across = many(level[1], level[0])
    bbuf[outer, 0] = pack(across[:BLK])
    bbuf[outer, 1] = pack(across[PAD : PAD + BLK])
    for t in reversed(outer_steps):
        hand(bbuf, (outer, core), t, b_send, b_recv, outer_peer(t))

    give(qbuf, q_send, q_recv)

    put(m_refs, span - 1, jnp.zeros((RIM, RIM), F32))
    put(r_refs, span - 1, eye)
    put(n_refs, 0, jnp.zeros((RIM, RIM), F32))
    put(p_refs, 0, eye)

    def chain(t, carry):
        s = span - 1 - t
        right = get(a_refs, s)
        put(m_refs, s - 1, many(get(m_refs, s), right) + flag(s == inner) * eye)
        put(r_refs, s - 1, many(get(r_refs, s), right))
        left = get(a_refs, t)
        put(n_refs, t + 1, many(left, get(n_refs, t)) + flag(t == inner) * eye)
        put(p_refs, t + 1, many(left, get(p_refs, t)))
        return carry

    lax.fori_loop(0, span - 1, chain, 0, unroll=True)

    far, local, back = forward_across(0, near, local)

    take(qbuf, q_send, q_recv, lambda s: None)
    halves = []
    for s in range(span):
        whole = jnp.concatenate([unpack(qbuf[s, 0]), unpack(qbuf[s, 1])], axis=0)
        halves.append(split(many(split(whole), get(p_refs, s)).T))
    entered = [
        sum(many(halves[s], get(refs, s)) for s in range(span)) for refs in (p_refs, n_refs)
    ]
    put(t_refs, 0, entered[0])
    put(t_refs, 1, entered[1])
    high, low = split(many((xh[:, :RIM], xl[:, :RIM]), get(p_refs, inner)))
    wh[...] = high
    wl[...] = low

    for t in outer_steps:
        origin = at_outer(-t)
        awaited(bbuf, (origin, core), t, b_send, b_recv)
        hand(bbuf, (origin, core), spans + t, b_send, b_recv, sibling)
    falling = backward_inside(back)
    take_in(bbuf, outer)
    for t in outer_steps:
        origin = at_outer(-t)
        awaited(bbuf, (origin, 1 - core), spans + t, b_send, b_recv)
        take_in(bbuf, origin)
    mine_r = rh[inner].astype(F32) + rl[inner].astype(F32)
    put(m2_refs, spans - 1, jnp.zeros((RIM, RIM), F32))
    put(n2_refs, 0, jnp.zeros((RIM, RIM), F32))

    def outer_chain(t, carry):
        s = spans - 1 - t
        put(m2_refs, s - 1, many(get(m2_refs, s), get(a_refs, s)) + flag(s == outer) * eye)
        put(n2_refs, t + 1, many(get(a_refs, t), get(n2_refs, t)) + flag(t == outer) * mine_r)
        return carry

    lax.fori_loop(0, spans - 1, outer_chain, 0, unroll=True)

    state, _, _ = forward_last(far, local, falling)
    direction, waiting = backward(0, state, place_system)
    image = system_times(0, direction)
    energy = total_of(waiting)
    answer = jnp.zeros_like(residual)

    def write(n, value):
        for i in range(ROWS):
            out_ref[n, i] = value[:, i * PAD : (i + 1) * PAD]

    for step in range(ITERS):
        phase = 5 * (step + 1)
        near, local = forward_local(phase, image, lane_sum(direction * image))
        last = step == ITERS - 1
        far, local, back = forward_across(phase, near, local, state[0] if last else None)
        falling = backward_inside(back)
        change, curvature, entering = forward_last(far, local, falling)
        alpha = energy / curvature
        part = None
        if last:
            received = falling[2]
            crossed = pick(received, 1) - lane_sum(state[1] * entering)
            squared = pick(received, 2) - lane_sum((falling[0] + change[1]) * entering)
            part = pick(received, 0) - alpha * (2.0 * crossed - alpha * squared)
        state = tuple(old - alpha * new for old, new in zip(state, change))
        held = []

        def settle():
            held.append(answer + alpha * direction)
            held.append(residual - alpha * image)
            if last:
                write(0, held[0])
                write(1, held[1])
                for copy in sends[:-1]:
                    copy.wait_send()
                del sends[:-1]

        precond, waiting = backward(phase, state, settle, part)
        answer, residual = held
        if not last:
            following = system_times(step + 1, precond)
        energy_next = waiting if last else total_of(waiting)
        ratio = energy_next / energy
        direction = precond + ratio * direction
        if not last:
            image = following + ratio * image
        energy = energy_next

    write(2, direction)
    for copy in sends:
        copy.wait_send()


def per_device(
    spans, cols, rhs, system_lower, system_diag, factor_lower, diag_inverse, neighbours, counts
):
    rows, width, columns = rhs.shape
    vmem = pl.BlockSpec(memory_space=pltpu.VMEM)
    phases = 5 * (ITERS + 1) - 1
    half = lambda: pltpu.VMEM((GROUP, RIM, RIM), BF16)
    most = max(GROUP, spans)
    tall = lambda: pltpu.VMEM((most, RIM, RIM), BF16)
    dma = pltpu.SemaphoreType.DMA
    outs = pl.pallas_call(
        functools.partial(kernel, GROUP, spans, cols),
        out_shape=jax.ShapeDtypeStruct((3, rows, columns, PAD), F32),
        in_specs=[pl.BlockSpec(memory_space=pltpu.SMEM)] * 2
        + [vmem, pl.BlockSpec(memory_space=pl.ANY)]
        + [vmem] * 3,
        out_specs=vmem,
        scratch_shapes=[
            pltpu.VMEM((WIDE, RIM + WIDE), F32),
            pltpu.VMEM((WIDE, RIM + WIDE), BF16),
            pltpu.VMEM((WIDE, RIM + WIDE), BF16),
            pltpu.VMEM((WIDE, RIM + WIDE), BF16),
            pltpu.VMEM((WIDE, RIM + WIDE), BF16),
            pltpu.VMEM((ROWS, PAD, PAD), BF16),
            pltpu.VMEM((ROWS, PAD, PAD), BF16),
            pltpu.VMEM((cols,) + system_lower.shape, F32),
            pltpu.VMEM((GROUP, 2, PACKED, PAD), F32),
            pltpu.VMEM((spans, 2, PACKED, PAD), F32),
            pltpu.VMEM((GROUP, 2, PACKED, PAD), F32),
            tall(), tall(),
            pltpu.VMEM((2, RIM, RIM), BF16), pltpu.VMEM((2, RIM, RIM), BF16),
            pltpu.VMEM((WIDE, RIM), BF16), pltpu.VMEM((WIDE, RIM), BF16),
            half(), half(), half(), half(), half(), half(), half(), half(),
            tall(), tall(), tall(), tall(),
            pltpu.VMEM((phases, most, columns, RIM), F32),
            pltpu.VMEM((ITERS, 2, columns, RIM), F32),
            pltpu.VMEM((ITERS, 2, columns, RIM), F32),
            dma, dma, dma, dma((GROUP,)), dma((GROUP,)), dma((2 * spans,)), dma((2 * spans,)),
            dma((GROUP,)), dma((GROUP,)),
            dma((phases,)), dma((phases, most - 1)), dma((ITERS, 2)), dma((ITERS, 2)),
        ],
        compiler_params=pltpu.CompilerParams(
            collective_id=0, has_side_effects=True, vmem_limit_bytes=60 * 1024 * 1024
        ),
    )(
        neighbours, counts, jnp.transpose(rhs, (0, 2, 1)), system_lower, system_diag,
        factor_lower, diag_inverse,
    )
    return tuple(jnp.transpose(outs[n, :, :, :width], (0, 2, 1)) for n in range(3))


def solution(mesh):
    in_specs = (
        P("row", None, "col"),
        P("row", "col", None, None),
        P("row", None, None),
        P("row", None, None, None),
        P("row", None, None),
        P("row", None),
        P("row"),
    )
    out_specs = (P("row", None, "col"), P("row", None, "col"), P("row", None, "col"))
    return jax.shard_map(
        functools.partial(per_device, mesh.shape["row"] // GROUP, mesh.shape["col"]),
        mesh=mesh, in_specs=in_specs, out_specs=out_specs, check_vma=False,
    )
```
